256 devices in a mesh: batch: 32 (over y, x, core), feat: 8 (over z).
Axes of the slice: x: 4, y: 4, z: 8, core: 2. Of those that a mesh axis runs over, the one named last changes fastest.
Arguments:
- features: bfloat16 [262144, 1024], P('batch', 'feat'), may hold values from -6 to 6
- nbr_one: int32 [15, 65536], P(None, 'batch'), may hold values from 0 to 8191
- count_one: int32 [65536], P('batch'), may hold values from 1 to 15
- nbr_two: int32 [10, 16384], P(None, 'batch'), may hold values from 0 to 2047
- count_two: int32 [16384], P('batch'), may hold values from 1 to 10
- self_one: bfloat16 [1024, 512], P('feat'), may hold values from -0.1875 to 0.1875
- neigh_one: bfloat16 [1024, 512], P('feat'), may hold values from -0.1875 to 0.1875
- bias_one: float32 [512], replicated, may hold values from -3 to 3
- self_two: bfloat16 [512, 512], replicated, may hold values from -0.25 to 0.25
- neigh_two: bfloat16 [512, 512], replicated, may hold values from -0.25 to 0.25
- bias_two: float32 [512], replicated, may hold values from -3 to 3
- cotangent: bfloat16 [16384, 512], P(('batch', 'feat')), may hold values from -6 to 6
Outputs:
- grad_self_one: float32 [1024, 512], P('feat')
- grad_neigh_one: float32 [1024, 512], P('feat')
- grad_bias_one: float32 [512], replicated
- grad_self_two: float32 [512, 512], replicated
- grad_neigh_two: float32 [512, 512], replicated
- grad_bias_two: float32 [512], replicated
The draws below stay inside these ranges and needn't reach their ends.
Inputs may be any that keep to these rules, and one draw needn't show every extreme that they name: First count_one entries of a column are the valid ones. First count_two entries of a column are the valid ones. `nbr_one`: rows inside the mini-batch's own block of 8192 input rows. `nbr_two`: rows inside the mini-batch's own block of 2048 layer one nodes.
All inputs are finite; a program needn't handle non-finite values.
Results may differ from the reference program's by a relative error of at most 0.008.
Values may be sent and summed in bfloat16 or wider, within the bound.
A program may use at most 64 MiB of HBM per device.

```python
import jax
import jax.numpy as jnp
from jax import lax

FEATS = 1024
HIDDEN_SIZE = 512
FAN_ONE = 15
FAN_TWO = 10
SEEDS = 512
MIDDLE = 2048
SOURCES = 8192
N_BATCH = 32


def plant(array, own_key, least, top_value):
    shape = array.shape
    spot = [jax.random.randint(jax.random.fold_in(own_key, axis), (), 0, shape[axis]) for axis in range(len(shape))]
    array = array.at[tuple(spot)].set(least)
    longest = shape.index(max(shape))
    spot[longest] = (spot[longest] + 1) % shape[longest]
    return array.at[tuple(spot)].set(top_value)


def levels(stream_key, shape, shards, low, largest):
    loudness, own = 1.0, jax.random.fold_in(stream_key, 6)
    for dim, blocks in shards:
        steps = jnp.exp(jax.random.uniform(jax.random.fold_in(own, dim), (blocks,), jnp.float32, low / len(shards), largest / len(shards)))
        loudness = loudness * jnp.repeat(steps, shape[dim] // blocks).reshape([-1 if axis == dim else 1 for axis in range(len(shape))])
    return loudness


def gaussian(stream_key, extent, scale, limit, shards=(), kind=jnp.bfloat16):
    array = jax.random.normal(stream_key, extent, jnp.float32) * scale
    if len(shards) > 0:
        array = levels(stream_key, extent, shards, -0.22, 0.18) * array
    return jnp.clip(array, min=-limit, max=limit).astype(kind)


def setup_inputs(seed: int = 0) -> dict:
    seeds = jax.random.split(jax.random.key(seed), 13)
    features = gaussian(seeds[0], (SOURCES * N_BATCH, FEATS), 1.0, 6.0, ((0, 32), (1, 8)))
    nbr_one = plant(jax.random.randint(seeds[1], (FAN_ONE, MIDDLE * N_BATCH), 0, SOURCES), jax.random.fold_in(seeds[1], 1), 0, SOURCES - 1).astype(jnp.int32)
    count_one = plant(jax.random.randint(seeds[2], (MIDDLE * N_BATCH,), 1, FAN_ONE + 1), jax.random.fold_in(seeds[2], 1), 1, FAN_ONE).astype(jnp.int32)
    nbr_two = plant(jax.random.randint(seeds[3], (FAN_TWO, SEEDS * N_BATCH), 0, MIDDLE), jax.random.fold_in(seeds[3], 1), 0, MIDDLE - 1).astype(jnp.int32)
    count_two = plant(jax.random.randint(seeds[4], (SEEDS * N_BATCH,), 1, FAN_TWO + 1), jax.random.fold_in(seeds[4], 1), 1, FAN_TWO).astype(jnp.int32)
    self_one = gaussian(seeds[5], (FEATS, HIDDEN_SIZE), FEATS ** -0.5, 0.1875, ((0, 8),))
    neigh_one = gaussian(seeds[6], (FEATS, HIDDEN_SIZE), FEATS ** -0.5, 0.1875, ((0, 8),))
    bias_one = gaussian(seeds[7], (HIDDEN_SIZE,), 0.5, 3.0, (), jnp.float32)
    self_two = gaussian(seeds[8], (HIDDEN_SIZE, HIDDEN_SIZE), HIDDEN_SIZE ** -0.5, 0.25)
    neigh_two = gaussian(seeds[9], (HIDDEN_SIZE, HIDDEN_SIZE), HIDDEN_SIZE ** -0.5, 0.25)
    bias_two = gaussian(seeds[10], (HIDDEN_SIZE,), 0.5, 3.0, (), jnp.float32)
    cotangent = gaussian(seeds[11], (SEEDS * N_BATCH, HIDDEN_SIZE), 1.0, 6.0, ((0, 256),))
    return dict(features=features, nbr_one=nbr_one, count_one=count_one, nbr_two=nbr_two, count_two=count_two, self_one=self_one, neigh_one=neigh_one, bias_one=bias_one, self_two=self_two, neigh_two=neigh_two, bias_two=bias_two, cotangent=cotangent)


def neighbour_mean(table, index, count):
    total = jnp.zeros((index.shape[1], table.shape[1]), jnp.float32)
    for k in range(index.shape[0]):
        rows = jnp.take(table, index[k], axis=0).astype(jnp.float32)
        total = total + jnp.where((k < count)[:, None], rows, 0.0)
    return (total / count[:, None].astype(jnp.float32)).astype(jnp.bfloat16)


def reference(features, nbr_one, count_one, nbr_two, count_two, self_one, neigh_one, bias_one, self_two, neigh_two, bias_two, cotangent):
    def group(carry, number):
        block = lax.dynamic_slice_in_dim(features, number * SOURCES, SOURCES, 0)
        index_one = lax.dynamic_slice_in_dim(nbr_one, number * MIDDLE, MIDDLE, 1)
        cnt_one = lax.dynamic_slice_in_dim(count_one, number * MIDDLE, MIDDLE, 0)
        index_two = lax.dynamic_slice_in_dim(nbr_two, number * SEEDS, SEEDS, 1)
        cnt_two = lax.dynamic_slice_in_dim(count_two, number * SEEDS, SEEDS, 0)
        upward = lax.dynamic_slice_in_dim(cotangent, number * SEEDS, SEEDS, 0)
        mean_one = neighbour_mean(block, index_one, cnt_one)
        own_rows = block[:MIDDLE]
        pre_one = jnp.dot(own_rows, self_one, preferred_element_type=jnp.float32)
        pre_one = pre_one + jnp.dot(mean_one, neigh_one, preferred_element_type=jnp.float32)
        act_one = jax.nn.softplus(pre_one + bias_one).astype(jnp.bfloat16)
        mean_two = neighbour_mean(act_one, index_two, cnt_two)
        own_two = act_one[:SEEDS]
        pre_two = jnp.dot(own_two, self_two, preferred_element_type=jnp.float32)
        pre_two = pre_two + jnp.dot(mean_two, neigh_two, preferred_element_type=jnp.float32) + bias_two
        slope_two = (upward.astype(jnp.float32) * jax.nn.sigmoid(pre_two)).astype(jnp.bfloat16)
        g_self_two = jnp.dot(own_two.T, slope_two, preferred_element_type=jnp.float32)
        g_neigh_two = jnp.dot(mean_two.T, slope_two, preferred_element_type=jnp.float32)
        g_bias_two = jnp.sum(slope_two.astype(jnp.float32), axis=0)
        back_one = jnp.zeros((MIDDLE, HIDDEN_SIZE), jnp.float32)
        back_one = back_one.at[:SEEDS].add(jnp.dot(slope_two, self_two.T, preferred_element_type=jnp.float32))
        spread = jnp.dot(slope_two, neigh_two.T, preferred_element_type=jnp.float32) / cnt_two[:, None].astype(jnp.float32)
        for k in range(FAN_TWO):
            back_one = back_one.at[index_two[k]].add(jnp.where((k < cnt_two)[:, None], spread, 0.0))
        slope_one = (back_one * (1.0 - jnp.exp(-act_one.astype(jnp.float32)))).astype(jnp.bfloat16)
        g_self_one = jnp.dot(own_rows.T, slope_one, preferred_element_type=jnp.float32)
        g_neigh_one = jnp.dot(mean_one.T, slope_one, preferred_element_type=jnp.float32)
        g_bias_one = jnp.sum(slope_one.astype(jnp.float32), axis=0)
        parts = (g_self_one, g_neigh_one, g_bias_one, g_self_two, g_neigh_two, g_bias_two)
        return tuple(a + b for a, b in zip(carry, parts)), None

    start = (jnp.zeros((FEATS, HIDDEN_SIZE), jnp.float32), jnp.zeros((FEATS, HIDDEN_SIZE), jnp.float32), jnp.zeros((HIDDEN_SIZE,), jnp.float32),
             jnp.zeros((HIDDEN_SIZE, HIDDEN_SIZE), jnp.float32), jnp.zeros((HIDDEN_SIZE, HIDDEN_SIZE), jnp.float32), jnp.zeros((HIDDEN_SIZE,), jnp.float32))
    result, unused = lax.scan(group, start, jnp.arange(N_BATCH, dtype=jnp.int32))
    return (result[0], result[1], result[2], result[3], result[4], result[5])
```

```python
import functools

import jax
import jax.numpy as jnp
from jax import lax
from jax.experimental import pallas as pl
from jax.experimental.pallas import tpu as pltpu
from jax.sharding import PartitionSpec as P

MESH = pl.DeviceIdType.MESH
F32 = jnp.float32
BF16 = jnp.bfloat16
VMEM = pl.BlockSpec(memory_space=pltpu.VMEM)
SMEM = pl.BlockSpec(memory_space=pltpu.SMEM)
ANY = pl.BlockSpec(memory_space=pl.ANY)

SOURCES = 8192
MIDDLE = 2048
SEEDS = 512
HID = 512
COLS = 128
FAN_ONE = 15
FAN_TWO = 10
Z = 8
OWN = 256
OWN_SEEDS = 64
REST = 192
GROUP = 32


def tree_sum(terms):
    while len(terms) > 1:
        odd = [terms[-1]] if len(terms) % 2 else []
        terms = [a + b for a, b in zip(terms[::2], terms[1::2])] + odd
    return terms[0]


def mean_kernel(index_ref, inverse_ref, features_ref, mean_ref, table, total):
    def widen(i, carry):
        rows = pl.ds(pl.multiple_of(i * 256, 256), 256)
        table[rows, :] = features_ref[rows, :].astype(F32)
        return carry

    lax.fori_loop(0, SOURCES // 256, widen, 0)
    table[pl.ds(SOURCES, 8), :] = jnp.zeros((8, COLS), F32)

    def step(g, carry):
        block, part = g // 8, g % 8
        seed_base = block * OWN_SEEDS + part * GROUP
        rest_base = SEEDS + block * REST + (part - 2) * GROUP
        base = jnp.where(part < 2, seed_base, rest_base)
        out = pl.multiple_of(g * GROUP, GROUP)
        for j in range(GROUP):
            rows = [table[pl.ds(index_ref[k, base + j], 1), :] for k in range(FAN_ONE)]
            total[pl.ds(out + j, 1), :] = tree_sum(rows) * inverse_ref[base + j]
        return carry

    lax.fori_loop(0, MIDDLE // GROUP, step, 0)

    def narrow(i, carry):
        rows = pl.ds(pl.multiple_of(i * 256, 256), 256)
        mean_ref[rows, :] = total[rows, :].astype(BF16)
        return carry

    lax.fori_loop(0, MIDDLE // 256, narrow, 0)


def mean_in_blocks(index, inverse, features):
    return pl.pallas_call(
        mean_kernel,
        name="mean_one",
        out_shape=jax.ShapeDtypeStruct((MIDDLE, COLS), BF16),
        in_specs=[SMEM, SMEM, VMEM],
        out_specs=VMEM,
        scratch_shapes=[
            pltpu.VMEM((SOURCES + 8, COLS), F32),
            pltpu.VMEM((MIDDLE, COLS), F32),
        ],
        compiler_params=pltpu.CompilerParams(vmem_limit_bytes=32 << 20),
        cost_estimate=pl.CostEstimate(flops=60_000_000_000, bytes_accessed=3_000_000, transcendentals=0),
    )(index, inverse, features)


def dot(a, b):
    return jnp.dot(a, b, preferred_element_type=F32)


def dot_tn(a, b):
    return lax.dot_general(a, b, (((0,), (0,)), ((), ())), preferred_element_type=F32)


def dot_nt(a, b):
    return lax.dot_general(a, b, (((1,), (1,)), ((), ())), preferred_element_type=F32)


N_COPIES = 200


def step_kernel(
    features,
    mean_ref,
    self_one,
    neigh_one,
    bias_one,
    self_two,
    neigh_two,
    bias_two,
    cotangent,
    index_two,
    inverse_two,
    out_one,
    out_two,
    out_bias,
    own_in,
    act_own,
    act_cols,
    weights,
    mean_send,
    mean_land,
    mean_two,
    slope_two,
    spread_send,
    spread_cols,
    direct,
    scat_send,
    scat_own,
    slope_one,
    g2_keep,
    g2_send,
    g2_core,
    g2_sum,
    g2_plane,
    g2_piece,
    g2_z,
    g2_row,
    g1_keep,
    g1_send,
    g1_core,
    g1_sum,
    g1_plane,
    g1_piece,
    g1_z,
    bias_mine,
    bias_core,
    bias_pair,
    bias_plane,
    bias_chips,
    bias_z,
    send_sem,
    recv_sem,
    local_sem,
):
    b = lax.axis_index("batch")
    z = lax.axis_index("feat")
    core = b % 2
    x = (b // 2) % 4
    y = b // 8
    half = z // 4
    col = z % 4
    chip = y * 4 + x
    other = 1 - core
    sibling = {"batch": b + 1 - 2 * core, "feat": z}
    z_peers = [(z + d) % Z for d in range(1, Z)]
    half_peers = [(col + d) % 4 for d in range(1, 4)]
    plane_peers = [((x + d % 4) % 4, (y + d // 4) % 4) for d in range(1, 16)]

    def at_z(peer):
        return {"batch": b, "feat": peer}

    def at_plane(peer):
        return {"batch": peer[1] * 8 + peer[0] * 2 + core, "feat": z}

    used = []

    def send(src, dst, device):
        number = len(used)
        used.append(number)
        copy = pltpu.make_async_remote_copy(
            src_ref=src,
            dst_ref=dst,
            send_sem=send_sem.at[number],
            recv_sem=recv_sem.at[number],
            device_id=device,
            device_id_type=MESH,
        )
        copy.start()
        return copy

    def wait(copies):
        for copy in copies:
            copy.wait()

    def lanes(number, start=0):
        return pl.ds(pl.multiple_of(start + number * 128, 128), 128)

    def rows(number, size, start=0):
        return pl.ds(pl.multiple_of(start + number * size, 16), size)

    barrier = pltpu.get_barrier_semaphore()
    everyone = [at_z(p) for p in z_peers] + [at_plane(p) for p in plane_peers] + [sibling]
    for device in everyone:
        pl.semaphore_signal(barrier, inc=1, device_id=device, device_id_type=MESH)
    own_a = pltpu.make_async_copy(
        features.at[rows(z, OWN_SEEDS), :], own_in.at[pl.ds(0, OWN_SEEDS), lanes(z)], local_sem.at[0]
    )
    own_b = pltpu.make_async_copy(
        features.at[rows(z, REST, SEEDS), :], own_in.at[pl.ds(OWN_SEEDS, REST), lanes(z)], local_sem.at[1]
    )
    own_a.start()
    own_b.start()
    own_in[:, lanes(z, 1024)] = mean_ref[rows(z, OWN), :]
    pl.semaphore_wait(barrier, len(everyone))

    pending_mean = [
        send(mean_ref.at[rows(p, OWN), :], own_in.at[:, lanes(z, 1024)], at_z(p)) for p in z_peers
    ]
    pending_own = []
    for p in z_peers:
        pending_own.append(
            send(features.at[rows(p, OWN_SEEDS), :], own_in.at[pl.ds(0, OWN_SEEDS), lanes(z)], at_z(p))
        )
        pending_own.append(
            send(
                features.at[rows(p, REST, SEEDS), :],
                own_in.at[pl.ds(OWN_SEEDS, REST), lanes(z)],
                at_z(p),
            )
        )

    def count_block(i, carry):
        spot = lax.broadcasted_iota(jnp.int32, (64, SEEDS), 0) + (i % 4) * 64
        block = half * 4 + i // 4
        node = jnp.where(spot < OWN_SEEDS, block * OWN_SEEDS + spot, SEEDS - OWN_SEEDS + block * REST + spot)
        total = jnp.zeros((64, SEEDS), F32)
        for k in range(FAN_TWO):
            total = total + jnp.where(node == index_two[k : k + 1, :], 1.0, 0.0)
        weights[rows(i, 64), :] = total.astype(BF16)
        return carry

    lax.fori_loop(0, 16, count_block, 0)

    own_a.wait()
    own_b.wait()
    wait(pending_mean)
    wait(pending_own)

    def layer_one(n, carry):
        cols = pl.ds(pl.multiple_of(n * 256, 256), 256)
        pre = dot(own_in[:, pl.ds(0, 1024)], self_one[:, cols])
        pre = pre + dot(own_in[:, pl.ds(1024, 1024)], neigh_one[:, cols]) + bias_one[:, cols]
        act_own[:, cols] = jax.nn.softplus(pre).astype(BF16)
        return carry

    lax.fori_loop(0, 2, layer_one, 0)

    pending = [
        send(act_own.at[:, lanes(p)], act_cols.at[rows(col, OWN), :], at_z(half * 4 + p)) for p in half_peers
    ]
    act_cols[rows(col, OWN), :] = act_own[:, lanes(col)]
    wait(pending)

    share = dot_tn(act_cols[...], weights[...])
    mean_send[...] = (share.T * inverse_two[...]).astype(BF16)
    pending = [send(mean_send.at[rows(p, OWN_SEEDS), :], mean_land.at[z], at_z(p)) for p in z_peers]
    mean_land[z] = mean_send[rows(z, OWN_SEEDS), :]
    pre_self = dot(act_own[pl.ds(0, OWN_SEEDS), :], self_two[...]) + bias_two[...]
    wait(pending)
    for q in range(4):
        both = mean_land[q].astype(F32) + mean_land[4 + q].astype(F32)
        mean_two[:, q * 128 : (q + 1) * 128] = both.astype(BF16)

    pre_two = pre_self + dot(mean_two[...], neigh_two[...])
    slope = cotangent[...].astype(F32) * jax.nn.sigmoid(pre_two)
    slope_two[...] = slope.astype(BF16)

    spread = dot_nt(slope_two[...], neigh_two[...])
    inverse = inverse_two[rows(z, OWN_SEEDS), :]
    for q in range(4):
        cols = slice(q * 128, (q + 1) * 128)
        spread_send[:, cols] = (spread[:, cols] * inverse).astype(BF16)
    pending = [
        send(spread_send.at[:, lanes(p % 4)], spread_cols.at[rows(z, OWN_SEEDS), :], at_z(p)) for p in z_peers
    ]
    spread_cols[rows(z, OWN_SEEDS), :] = spread_send[:, lanes(col)]

    own_two = act_own[pl.ds(0, OWN_SEEDS), :]
    keep_self = jnp.where(core == 0, 1.0, 0.0).astype(BF16)
    keep_neigh = jnp.where(core == 0, 0.0, 1.0).astype(BF16)
    mixed_send = own_two * keep_neigh + mean_two[...] * keep_self
    mixed_keep = own_two * keep_self + mean_two[...] * keep_neigh
    g2_send[...] = dot_tn(mixed_send, slope_two[...]).astype(BF16)
    pending_g2 = [send(g2_send, g2_core, sibling)]
    g2_keep[...] = dot_tn(mixed_keep, slope_two[...])

    def direct_block(n, carry):
        cols = pl.ds(pl.multiple_of(n * 256, 256), 256)
        direct[:, cols] = dot_nt(slope_two[...], self_two[cols, :])
        return carry

    lax.fori_loop(0, 2, direct_block, 0)
    bias_two_sum = jnp.sum(slope_two[...].astype(F32), axis=0, keepdims=True)
    wait(pending)

    def scatter_block(i, carry):
        block = rows(i, OWN)
        scat_send[block, :] = dot(weights[block, :], spread_cols[...]).astype(BF16)
        return carry

    lax.fori_loop(0, 4, scatter_block, 0)
    pending = [
        send(scat_send.at[rows(p, OWN), :], scat_own.at[:, lanes(col)], at_z(half * 4 + p)) for p in half_peers
    ]
    scat_own[:, lanes(col)] = scat_send[rows(col, OWN), :]
    wait(pending_g2)

    def g2_pair(i, carry):
        block = rows(i, 128)
        g2_sum[block, :] = (g2_keep[block, :] + g2_core[block, :].astype(F32)).astype(BF16)
        return carry

    lax.fori_loop(0, 4, g2_pair, 0)
    pending_g2 = [
        send(g2_sum.at[rows(p[1], 128), lanes(p[0])], g2_plane.at[chip], at_plane(p)) for p in plane_peers
    ]
    g2_plane[chip] = g2_sum[rows(y, 128), lanes(x)]
    wait(pending)

    back = scat_own[pl.ds(0, OWN_SEEDS), :].astype(F32) + direct[...]
    gate = 1.0 - jnp.exp(-act_own[pl.ds(0, OWN_SEEDS), :].astype(F32))
    slope_one[pl.ds(0, OWN_SEEDS), :] = (back * gate).astype(BF16)
    back = scat_own[pl.ds(OWN_SEEDS, REST), :].astype(F32)
    gate = 1.0 - jnp.exp(-act_own[pl.ds(OWN_SEEDS, REST), :].astype(F32))
    slope_one[pl.ds(OWN_SEEDS, REST), :] = (back * gate).astype(BF16)

    def g1_block(t, carry):
        g1_send[t] = dot_tn(own_in[:, lanes(t, other * 1024)], slope_one[...]).astype(BF16)
        return carry

    pending = []
    for part in range(2):
        lax.fori_loop(part * 4, part * 4 + 4, g1_block, 0)
        chunk = pl.ds(part * 4, 4)
        pending.append(send(g1_send.at[chunk], g1_core.at[chunk], sibling))
    bias_one_sum = jnp.sum(slope_one[...].astype(F32), axis=0, keepdims=True)
    for i in range(4):
        bias_mine[i : i + 1, :] = bias_one_sum[:, i * 128 : (i + 1) * 128]
        bias_mine[4 + i : 5 + i, :] = bias_two_sum[:, i * 128 : (i + 1) * 128]
    pending_bias = [send(bias_mine, bias_core, sibling)]

    def g1_own(t, carry):
        g1_keep[t] = dot_tn(own_in[:, lanes(t, core * 1024)], slope_one[...])
        return carry

    lax.fori_loop(0, 8, g1_own, 0)
    wait(pending_bias)
    bias_pair[...] = bias_mine[...] + bias_core[...]
    wait(pending)

    def g1_pair(t, carry):
        both = g1_keep[t] + g1_core[t].astype(F32)
        g1_sum[t] = both.astype(BF16).reshape(4, 32, HID)
        return carry

    lax.fori_loop(0, 8, g1_pair, 0)

    pending = [
        send(g1_sum.at[:, p[1], :, lanes(p[0])], g1_plane.at[chip], at_plane(p)) for p in plane_peers
    ]
    pending_bias = [send(bias_pair, bias_plane.at[chip], at_plane(p)) for p in plane_peers]
    g1_plane[chip] = g1_sum[:, y, :, lanes(x)]
    bias_plane[chip] = bias_pair[...]

    wait(pending_g2)
    total = tree_sum([g2_plane[p].astype(F32) for p in range(16)])
    g2_piece[...] = total.astype(BF16)
    pending_g2 = [send(g2_piece.at[rows(p, 16), :], g2_z.at[z], at_z(p)) for p in z_peers]
    g2_z[z] = g2_piece[rows(z, 16), :]
    wait(pending_g2)
    total = tree_sum([g2_z[p].astype(F32) for p in range(Z)])
    g2_row[rows(z, 16), :] = total.astype(BF16)
    pending_g2 = [send(g2_row.at[rows(z, 16), :], g2_row.at[rows(z, 16), :], at_z(p)) for p in z_peers]
    wait(pending_g2)

    wait(pending)

    def g1_chips(t, carry):
        total = tree_sum([g1_plane[p, t].astype(F32) for p in range(16)])
        g1_piece[t] = total.astype(BF16)
        return carry

    lax.fori_loop(0, 8, g1_chips, 0)
    pending = [send(g1_piece.at[p], g1_z.at[z], at_z(p)) for p in z_peers]
    g1_z[z] = g1_piece[z]
    pending_g2 = [
        send(g2_row, out_two.at[core, rows(y, 128), lanes(x)], at_plane(p)) for p in plane_peers
    ]
    out_two[core, rows(y, 128), lanes(x)] = g2_row[...]
    wait(pending_bias)
    bias_chips[...] = tree_sum([bias_plane[p] for p in range(16)])
    pending_bias = [send(bias_chips, bias_z.at[z], at_z(p)) for p in z_peers]
    bias_z[z] = bias_chips[...]
    wait(pending)
    total = tree_sum([g1_z[p].astype(F32) for p in range(Z)])
    out_one[core, rows(y, 32), lanes(x)] = total.astype(BF16)

    mine = out_one.at[core, rows(y, 32), lanes(x)]
    pending = [send(mine, mine, at_plane(p)) for p in plane_peers]
    wait(pending_g2)
    pending_g2 = [send(out_two.at[core], out_two.at[core], sibling)]
    wait(pending_bias)
    out_bias[...] = tree_sum([bias_z[p] for p in range(Z)])
    wait(pending)
    pending = [send(out_one.at[core], out_one.at[core], sibling)]
    wait(pending_g2)
    wait(pending)
    assert len(used) <= N_COPIES


def training_step(*operands):
    bf16 = [
        (OWN, 2 * Z * COLS),
        (OWN, HID),
        (4 * OWN, 128),
        (4 * OWN, SEEDS),
        (SEEDS, 128),
        (Z, OWN_SEEDS, 128),
        (OWN_SEEDS, HID),
        (OWN_SEEDS, HID),
        (OWN_SEEDS, HID),
        (SEEDS, 128),
        None,
        (4 * OWN, 128),
        (OWN, HID),
        (OWN, HID),
        None,
        (HID, HID),
        (HID, HID),
        (HID, HID),
        (16, 128, 128),
        (128, 128),
        (Z, 16, 128),
        (128, 128),
        None,
        (Z, 128, HID),
        (Z, 128, HID),
        (Z, 4, 32, HID),
        (16, Z, 32, 128),
        (Z, 32, 128),
        (Z, 32, 128),
    ]
    wide = iter([(OWN_SEEDS, HID), (HID, HID), (Z, 128, HID)])
    scratch = [pltpu.VMEM(s, BF16) if s else pltpu.VMEM(next(wide), F32) for s in bf16]
    tile = (8, 128)
    scratch += [pltpu.VMEM(s, F32) for s in (tile, tile, tile, (16, *tile), tile, (Z, *tile))]
    scratch += [pltpu.SemaphoreType.DMA((N_COPIES,)), pltpu.SemaphoreType.DMA((N_COPIES,))]
    scratch += [pltpu.SemaphoreType.DMA((2,))]
    return pl.pallas_call(
        step_kernel,
        name="training_step",
        out_shape=(
            jax.ShapeDtypeStruct((2, 128, HID), BF16),
            jax.ShapeDtypeStruct((2, HID, HID), BF16),
            jax.ShapeDtypeStruct(tile, F32),
        ),
        in_specs=[ANY] + [VMEM] * (len(operands) - 1),
        out_specs=(VMEM, VMEM, VMEM),
        scratch_shapes=scratch,
        compiler_params=pltpu.CompilerParams(
            collective_id=0, has_side_effects=True, vmem_limit_bytes=48 << 20
        ),
    )(*operands)


def on_device(
    features,
    nbr_one,
    count_one,
    nbr_two,
    count_two,
    self_one,
    neigh_one,
    bias_one,
    self_two,
    neigh_two,
    bias_two,
    cotangent,
):
    self_all = lax.all_gather(self_one, "feat", axis=0, tiled=True)
    neigh_all = lax.all_gather(neigh_one, "feat", axis=0, tiled=True)
    slot = lax.broadcasted_iota(jnp.int32, nbr_one.shape, 0)
    index_one = jnp.where(slot < count_one[None, :], nbr_one, SOURCES)
    mean_one = mean_in_blocks(index_one, 1.0 / count_one.astype(F32), features)
    slot = lax.broadcasted_iota(jnp.int32, nbr_two.shape, 0)
    index_two = jnp.where(slot < count_two[None, :], nbr_two, -1)
    inverse_two = jnp.broadcast_to(1.0 / count_two.astype(F32)[:, None], (SEEDS, 128))
    one, two, bias = training_step(
        features,
        mean_one,
        self_all,
        neigh_all,
        bias_one[None, :],
        self_two,
        neigh_two,
        bias_two[None, :],
        cotangent,
        index_two,
        inverse_two,
    )
    one, two = one.astype(F32), two.astype(F32)
    return one[0], one[1], bias[:4].reshape(HID), two[0], two[1], bias[4:].reshape(HID)


def solution(mesh):
    in_specs = (
        P("batch", "feat"),
        P(None, "batch"),
        P("batch"),
        P(None, "batch"),
        P("batch"),
        P("feat", None),
        P("feat", None),
        P(),
        P(),
        P(),
        P(),
        P(("batch", "feat"), None),
    )
    out_specs = (P("feat", None), P("feat", None), P(), P(), P(), P())
    return jax.shard_map(
        on_device, mesh=mesh, in_specs=in_specs, out_specs=out_specs, check_vma=False
    )
```

```python
import functools

import jax
import jax.numpy as jnp
from jax import lax
from jax.experimental import pallas as pl
from jax.experimental.pallas import tpu as pltpu
from jax.sharding import PartitionSpec as P

MESH = pl.DeviceIdType.MESH
F32 = jnp.float32
BF16 = jnp.bfloat16
VMEM = pl.BlockSpec(memory_space=pltpu.VMEM)
SMEM = pl.BlockSpec(memory_space=pltpu.SMEM)

SOURCES = 8192
MIDDLE = 2048
SEEDS = 512
HID = 512
COLS = 128
FAN_ONE = 15
FAN_TWO = 10
Z = 8
OWN = 256
OWN_SEEDS = 64
REST = 192
GROUP = 32


def tree_sum(terms):
    while len(terms) > 1:
        odd = [terms[-1]] if len(terms) % 2 else []
        terms = [a + b for a, b in zip(terms[::2], terms[1::2])] + odd
    return terms[0]


def dot(a, b):
    return jnp.dot(a, b, preferred_element_type=F32)


def dot_tn(a, b):
    return lax.dot_general(a, b, (((0,), (0,)), ((), ())), preferred_element_type=F32)


def dot_nt(a, b):
    return lax.dot_general(a, b, (((1,), (1,)), ((), ())), preferred_element_type=F32)


N_COPIES = 200


def step_kernel(
    index_one,
    inverse_one,
    features,
    self_one,
    neigh_one,
    bias_one,
    self_two,
    neigh_two,
    bias_two,
    cotangent,
    index_two,
    inverse_two,
    out_one,
    out_two,
    out_bias,
    table,
    total_one,
    mean_one,
    weights_mine,
    weights_one,
    own_in,
    act_own,
    act_cols,
    counts,
    mean_send,
    mean_land,
    mean_two,
    slope_two,
    spread_send,
    spread_cols,
    direct,
    scat_send,
    scat_own,
    slope_one,
    g2_keep,
    g2_send,
    g2_core,
    g2_sum,
    g2_plane,
    g2_piece,
    g2_z,
    g2_row,
    g1_keep,
    g1_send,
    g1_core,
    g1_sum,
    g1_plane,
    g1_piece,
    g1_z,
    bias_mine,
    bias_core,
    bias_pair,
    bias_plane,
    bias_chips,
    bias_z,
    send_sem,
    recv_sem,
):
    b = lax.axis_index("batch")
    z = lax.axis_index("feat")
    core = b % 2
    x = (b // 2) % 4
    y = b // 8
    half = z // 4
    col = z % 4
    chip = y * 4 + x
    other = 1 - core
    sibling = {"batch": b + 1 - 2 * core, "feat": z}
    z_peers = [(z + d) % Z for d in range(1, Z)]
    half_peers = [(col + d) % 4 for d in range(1, 4)]
    plane_peers = [((x + d % 4) % 4, (y + d // 4) % 4) for d in range(1, 16)]

    def at_z(peer):
        return {"batch": b, "feat": peer}

    def at_plane(peer):
        return {"batch": peer[1] * 8 + peer[0] * 2 + core, "feat": z}

    used = []

    def send(src, dst, device):
        number = len(used)
        used.append(number)
        copy = pltpu.make_async_remote_copy(
            src_ref=src,
            dst_ref=dst,
            send_sem=send_sem.at[number],
            recv_sem=recv_sem.at[number],
            device_id=device,
            device_id_type=MESH,
        )
        copy.start()
        return copy

    def wait(copies):
        for copy in copies:
            copy.wait()

    def lanes(number, start=0):
        return pl.ds(pl.multiple_of(start + number * 128, 128), 128)

    def rows(number, size, start=0):
        return pl.ds(pl.multiple_of(start + number * size, 16), size)

    barrier = pltpu.get_barrier_semaphore()
    everyone = [at_z(p) for p in z_peers] + [at_plane(p) for p in plane_peers] + [sibling]
    for device in everyone:
        pl.semaphore_signal(barrier, inc=1, device_id=device, device_id_type=MESH)
    def widen(i, carry):
        block = pl.ds(pl.multiple_of(i * 256, 256), 256)
        table[block, :] = features[block, :].astype(F32)
        return carry

    lax.fori_loop(0, SOURCES // 256, widen, 0)
    table[pl.ds(SOURCES, 8), :] = jnp.zeros((8, COLS), F32)
    weights_mine[pl.ds(0, COLS), :] = self_one[...]
    weights_mine[pl.ds(COLS, COLS), :] = neigh_one[...]
    own_in[pl.ds(0, OWN_SEEDS), lanes(2 * z)] = features[rows(z, OWN_SEEDS), :]
    own_in[pl.ds(OWN_SEEDS, REST), lanes(2 * z)] = features[rows(z, REST, SEEDS), :]
    cols_mine = pl.ds(pl.multiple_of(core * 256, 256), 256)
    weights_one[z, rows(chip, 16), cols_mine] = weights_mine[rows(chip, 16), cols_mine]
    pl.semaphore_wait(barrier, len(everyone))

    part = weights_one.at[z, rows(chip, 16), cols_mine]
    pending_weights = [send(weights_mine.at[rows(chip, 16), cols_mine], part, at_z(p)) for p in z_peers]
    pending_own = []
    for p in z_peers:
        pending_own.append(
            send(features.at[rows(p, OWN_SEEDS), :], own_in.at[pl.ds(0, OWN_SEEDS), lanes(2 * z)], at_z(p))
        )
        pending_own.append(
            send(
                features.at[rows(p, REST, SEEDS), :],
                own_in.at[pl.ds(OWN_SEEDS, REST), lanes(2 * z)],
                at_z(p),
            )
        )

    for turn, d in enumerate((4, 3, 5, 2, 6, 1, 7, 0)):
        owner = (z + d) % Z

        def gather(g, carry, owner=owner):
            seed_base = owner * OWN_SEEDS + g * GROUP
            rest_base = SEEDS - OWN_SEEDS + owner * REST + g * GROUP
            base = jnp.where(g < OWN_SEEDS // GROUP, seed_base, rest_base)
            out = pl.multiple_of(g * GROUP, GROUP)
            for j in range(GROUP):
                terms = [table[pl.ds(index_one[base + (k * MIDDLE + j)], 1), :] for k in range(FAN_ONE)]
                total_one[pl.ds(out + j, 1), :] = tree_sum(terms) * inverse_one[base + j]
            return carry

        lax.fori_loop(0, OWN // GROUP, gather, 0)
        if d:
            mean_one[turn] = total_one[...].astype(BF16)
            pending_own.append(send(mean_one.at[turn], own_in.at[:, lanes(2 * z + 1)], at_z(owner)))
        else:
            own_in[:, lanes(2 * z + 1)] = total_one[...].astype(BF16)
        if turn == 0:
            wait(pending_weights)
            part = weights_one.at[:, rows(chip, 16), cols_mine]
            pending_weights = [send(part, part, at_plane(p)) for p in plane_peers]
        if turn == 4:
            wait(pending_weights)
            part = weights_one.at[:, :, cols_mine]
            pending_weights = [send(part, part, sibling)]
    wait(pending_weights)
    wait(pending_own)

    def layer_one(n, carry):
        cols = pl.ds(pl.multiple_of(n * 256, 256), 256)
        pre = dot(own_in[...], weights_one[:, :, cols].reshape(2 * Z * COLS, 256)) + bias_one[:, cols]
        act_own[:, cols] = jax.nn.softplus(pre).astype(BF16)
        return carry

    lax.fori_loop(0, 2, layer_one, 0)

    pending = [
        send(act_own.at[:, lanes(p)], act_cols.at[rows(col, OWN), :], at_z(half * 4 + p)) for p in half_peers
    ]
    act_cols[rows(col, OWN), :] = act_own[:, lanes(col)]

    def count_block(i, carry):
        spot = lax.broadcasted_iota(jnp.int32, (64, SEEDS), 0) + (i % 4) * 64
        block = half * 4 + i // 4
        node = jnp.where(spot < OWN_SEEDS, block * OWN_SEEDS + spot, SEEDS - OWN_SEEDS + block * REST + spot)
        total = jnp.zeros((64, SEEDS), F32)
        for k in range(FAN_TWO):
            total = total + jnp.where(node == index_two[k : k + 1, :], 1.0, 0.0)
        counts[rows(i, 64), :] = total.astype(BF16)
        return carry

    lax.fori_loop(0, 16, count_block, 0)
    wait(pending)

    share = dot_tn(act_cols[...], counts[...])
    mean_send[...] = (share.T * inverse_two[...]).astype(BF16)
    pending = [send(mean_send.at[rows(p, OWN_SEEDS), :], mean_land.at[z], at_z(p)) for p in z_peers]
    mean_land[z] = mean_send[rows(z, OWN_SEEDS), :]
    pre_self = dot(act_own[pl.ds(0, OWN_SEEDS), :], self_two[...]) + bias_two[...]
    wait(pending)
    for q in range(4):
        both = mean_land[q].astype(F32) + mean_land[4 + q].astype(F32)
        mean_two[:, q * 128 : (q + 1) * 128] = both.astype(BF16)

    pre_two = pre_self + dot(mean_two[...], neigh_two[...])
    slope = cotangent[...].astype(F32) * jax.nn.sigmoid(pre_two)
    slope_two[...] = slope.astype(BF16)

    spread = dot_nt(slope_two[...], neigh_two[...])
    inverse = inverse_two[rows(z, OWN_SEEDS), :]
    for q in range(4):
        cols = slice(q * 128, (q + 1) * 128)
        spread_send[:, cols] = (spread[:, cols] * inverse).astype(BF16)
    pending = [
        send(spread_send.at[:, lanes(p % 4)], spread_cols.at[rows(z, OWN_SEEDS), :], at_z(p)) for p in z_peers
    ]
    spread_cols[rows(z, OWN_SEEDS), :] = spread_send[:, lanes(col)]

    own_two = act_own[pl.ds(0, OWN_SEEDS), :]
    keep_self = jnp.where(core == 0, 1.0, 0.0).astype(BF16)
    keep_neigh = jnp.where(core == 0, 0.0, 1.0).astype(BF16)
    mixed_send = own_two * keep_neigh + mean_two[...] * keep_self
    mixed_keep = own_two * keep_self + mean_two[...] * keep_neigh
    g2_send[...] = dot_tn(mixed_send, slope_two[...]).astype(BF16)
    pending_g2 = [send(g2_send, g2_core, sibling)]
    g2_keep[...] = dot_tn(mixed_keep, slope_two[...])

    def direct_block(n, carry):
        cols = pl.ds(pl.multiple_of(n * 256, 256), 256)
        direct[:, cols] = dot_nt(slope_two[...], self_two[cols, :])
        return carry

    lax.fori_loop(0, 2, direct_block, 0)
    bias_two_sum = jnp.sum(slope_two[...].astype(F32), axis=0, keepdims=True)
    wait(pending)

    def scatter_block(i, carry):
        block = rows(i, OWN)
        scat_send[block, :] = dot(counts[block, :], spread_cols[...]).astype(BF16)
        return carry

    lax.fori_loop(0, 4, scatter_block, 0)
    pending = [
        send(scat_send.at[rows(p, OWN), :], scat_own.at[:, lanes(col)], at_z(half * 4 + p)) for p in half_peers
    ]
    scat_own[:, lanes(col)] = scat_send[rows(col, OWN), :]
    wait(pending_g2)

    def g2_pair(i, carry):
        block = rows(i, 128)
        g2_sum[block, :] = (g2_keep[block, :] + g2_core[block, :].astype(F32)).astype(BF16)
        return carry

    lax.fori_loop(0, 4, g2_pair, 0)
    pending_g2 = [
        send(g2_sum.at[rows(p[1], 128), lanes(p[0])], g2_plane.at[chip], at_plane(p)) for p in plane_peers
    ]
    g2_plane[chip] = g2_sum[rows(y, 128), lanes(x)]
    wait(pending)

    back = scat_own[pl.ds(0, OWN_SEEDS), :].astype(F32) + direct[...]
    gate = 1.0 - jnp.exp(-act_own[pl.ds(0, OWN_SEEDS), :].astype(F32))
    slope_one[pl.ds(0, OWN_SEEDS), :] = (back * gate).astype(BF16)
    back = scat_own[pl.ds(OWN_SEEDS, REST), :].astype(F32)
    gate = 1.0 - jnp.exp(-act_own[pl.ds(OWN_SEEDS, REST), :].astype(F32))
    slope_one[pl.ds(OWN_SEEDS, REST), :] = (back * gate).astype(BF16)

    def g1_block(t, carry):
        g1_send[t] = dot_tn(own_in[:, lanes(2 * t + other)], slope_one[...]).astype(BF16)
        return carry

    pending = []
    for part in range(2):
        lax.fori_loop(part * 4, part * 4 + 4, g1_block, 0)
        chunk = pl.ds(part * 4, 4)
        pending.append(send(g1_send.at[chunk], g1_core.at[chunk], sibling))
    bias_one_sum = jnp.sum(slope_one[...].astype(F32), axis=0, keepdims=True)
    for i in range(4):
        bias_mine[i : i + 1, :] = bias_one_sum[:, i * 128 : (i + 1) * 128]
        bias_mine[4 + i : 5 + i, :] = bias_two_sum[:, i * 128 : (i + 1) * 128]
    pending_bias = [send(bias_mine, bias_core, sibling)]

    def g1_own(t, carry):
        g1_keep[t] = dot_tn(own_in[:, lanes(2 * t + core)], slope_one[...])
        return carry

    lax.fori_loop(0, 8, g1_own, 0)
    wait(pending_bias)
    bias_pair[...] = bias_mine[...] + bias_core[...]
    wait(pending)

    def g1_pair(t, carry):
        both = g1_keep[t] + g1_core[t].astype(F32)
        g1_sum[t] = both.astype(BF16).reshape(4, 32, HID)
        return carry

    lax.fori_loop(0, 8, g1_pair, 0)

    pending = [
        send(g1_sum.at[:, p[1], :, lanes(p[0])], g1_plane.at[chip], at_plane(p)) for p in plane_peers
    ]
    pending_bias = [send(bias_pair, bias_plane.at[chip], at_plane(p)) for p in plane_peers]
    g1_plane[chip] = g1_sum[:, y, :, lanes(x)]
    bias_plane[chip] = bias_pair[...]

    wait(pending_g2)
    total = tree_sum([g2_plane[p].astype(F32) for p in range(16)])
    g2_piece[...] = total.astype(BF16)
    pending_g2 = [send(g2_piece.at[rows(p, 16), :], g2_z.at[z], at_z(p)) for p in z_peers]
    g2_z[z] = g2_piece[rows(z, 16), :]
    wait(pending_g2)
    total = tree_sum([g2_z[p].astype(F32) for p in range(Z)])
    g2_row[rows(z, 16), :] = total.astype(BF16)
    pending_g2 = [send(g2_row.at[rows(z, 16), :], g2_row.at[rows(z, 16), :], at_z(p)) for p in z_peers]
    wait(pending_g2)

    wait(pending)

    def g1_chips(t, carry):
        total = tree_sum([g1_plane[p, t].astype(F32) for p in range(16)])
        g1_piece[t] = total.astype(BF16)
        return carry

    lax.fori_loop(0, 8, g1_chips, 0)
    pending = [send(g1_piece.at[p], g1_z.at[z], at_z(p)) for p in z_peers]
    g1_z[z] = g1_piece[z]
    pending_g2 = [
        send(g2_row, out_two.at[core, rows(y, 128), lanes(x)], at_plane(p)) for p in plane_peers
    ]
    out_two[core, rows(y, 128), lanes(x)] = g2_row[...]
    wait(pending_bias)
    bias_chips[...] = tree_sum([bias_plane[p] for p in range(16)])
    pending_bias = [send(bias_chips, bias_z.at[z], at_z(p)) for p in z_peers]
    bias_z[z] = bias_chips[...]
    wait(pending)
    total = tree_sum([g1_z[p].astype(F32) for p in range(Z)])
    out_one[core, rows(y, 32), lanes(x)] = total.astype(BF16)

    mine = out_one.at[core, rows(y, 32), lanes(x)]
    pending = [send(mine, mine, at_plane(p)) for p in plane_peers]
    wait(pending_g2)
    pending_g2 = [send(out_two.at[core], out_two.at[core], sibling)]
    wait(pending_bias)
    out_bias[...] = tree_sum([bias_z[p] for p in range(Z)])
    wait(pending)
    pending = [send(out_one.at[core], out_one.at[core], sibling)]
    wait(pending_g2)
    wait(pending)
    assert len(used) <= N_COPIES


def training_step(*operands):
    bf16 = [
        None,
        None,
        (Z - 1, OWN, COLS),
        (2 * COLS, HID),
        (Z, 2 * COLS, HID),
        (OWN, 2 * Z * COLS),
        (OWN, HID),
        (4 * OWN, 128),
        (4 * OWN, SEEDS),
        (SEEDS, 128),
        (Z, OWN_SEEDS, 128),
        (OWN_SEEDS, HID),
        (OWN_SEEDS, HID),
        (OWN_SEEDS, HID),
        (SEEDS, 128),
        None,
        (4 * OWN, 128),
        (OWN, HID),
        (OWN, HID),
        None,
        (HID, HID),
        (HID, HID),
        (HID, HID),
        (16, 128, 128),
        (128, 128),
        (Z, 16, 128),
        (128, 128),
        None,
        (Z, 128, HID),
        (Z, 128, HID),
        (Z, 4, 32, HID),
        (16, Z, 32, 128),
        (Z, 32, 128),
        (Z, 32, 128),
    ]
    wide = iter([(SOURCES + 8, COLS), (OWN, COLS), (OWN_SEEDS, HID), (HID, HID), (Z, 128, HID)])
    scratch = [pltpu.VMEM(s, BF16) if s else pltpu.VMEM(next(wide), F32) for s in bf16]
    tile = (8, 128)
    scratch += [pltpu.VMEM(s, F32) for s in (tile, tile, tile, (16, *tile), tile, (Z, *tile))]
    scratch += [pltpu.SemaphoreType.DMA((N_COPIES,)), pltpu.SemaphoreType.DMA((N_COPIES,))]
    return pl.pallas_call(
        step_kernel,
        name="training_step",
        out_shape=(
            jax.ShapeDtypeStruct((2, 128, HID), BF16),
            jax.ShapeDtypeStruct((2, HID, HID), BF16),
            jax.ShapeDtypeStruct(tile, F32),
        ),
        in_specs=[SMEM, SMEM] + [VMEM] * (len(operands) - 2),
        out_specs=(VMEM, VMEM, VMEM),
        scratch_shapes=scratch,
        compiler_params=pltpu.CompilerParams(
            collective_id=0, has_side_effects=True, vmem_limit_bytes=48 << 20
        ),
    )(*operands)


def on_device(
    features,
    nbr_one,
    count_one,
    nbr_two,
    count_two,
    self_one,
    neigh_one,
    bias_one,
    self_two,
    neigh_two,
    bias_two,
    cotangent,
):
    slot = lax.broadcasted_iota(jnp.int32, nbr_one.shape, 0)
    index_one = jnp.where(slot < count_one[None, :], nbr_one, SOURCES).reshape(-1)
    slot = lax.broadcasted_iota(jnp.int32, nbr_two.shape, 0)
    index_two = jnp.where(slot < count_two[None, :], nbr_two, -1)
    inverse_two = jnp.broadcast_to(1.0 / count_two.astype(F32)[:, None], (SEEDS, 128))
    one, two, bias = training_step(
        index_one,
        1.0 / count_one.astype(F32),
        features,
        self_one,
        neigh_one,
        bias_one[None, :],
        self_two,
        neigh_two,
        bias_two[None, :],
        cotangent,
        index_two,
        inverse_two,
    )
    one, two = one.astype(F32), two.astype(F32)
    return one[0], one[1], bias[:4].reshape(HID), two[0], two[1], bias[4:].reshape(HID)


def solution(mesh):
    in_specs = (
        P("batch", "feat"),
        P(None, "batch"),
        P("batch"),
        P(None, "batch"),
        P("batch"),
        P("feat", None),
        P("feat", None),
        P(),
        P(),
        P(),
        P(),
        P(("batch", "feat"), None),
    )
    out_specs = (P("feat", None), P("feat", None), P(), P(), P(), P())
    return jax.shard_map(
        on_device, mesh=mesh, in_specs=in_specs, out_specs=out_specs, check_vma=False
    )
```

```python
import functools

import jax
import jax.numpy as jnp
from jax import lax
from jax.experimental import pallas as pl
from jax.experimental.pallas import tpu as pltpu
from jax.sharding import PartitionSpec as P

MESH = pl.DeviceIdType.MESH
F32 = jnp.float32
BF16 = jnp.bfloat16
VMEM = pl.BlockSpec(memory_space=pltpu.VMEM)
SMEM = pl.BlockSpec(memory_space=pltpu.SMEM)
HBM = pl.BlockSpec(memory_space=pltpu.HBM)

SOURCES = 8192
MIDDLE = 2048
SEEDS = 512
HID = 512
COLS = 128
FAN_ONE = 15
FAN_TWO = 10
Z = 8
OWN = 256
OWN_SEEDS = 64
REST = 192
GROUP = 32


def tree_sum(terms):
    while len(terms) > 1:
        odd = [terms[-1]] if len(terms) % 2 else []
        terms = [a + b for a, b in zip(terms[::2], terms[1::2])] + odd
    return terms[0]


def dot(a, b):
    return jnp.dot(a, b, preferred_element_type=F32)


def dot_tn(a, b):
    return lax.dot_general(a, b, (((0,), (0,)), ((), ())), preferred_element_type=F32)


def dot_nt(a, b):
    return lax.dot_general(a, b, (((1,), (1,)), ((), ())), preferred_element_type=F32)


N_COPIES = 200


def step_kernel(
    index_one,
    features_in,
    count_one_in,
    self_one,
    neigh_one,
    bias_one_in,
    self_two_in,
    neigh_two_in,
    bias_two_in,
    cotangent_in,
    nbr_two_in,
    count_two_in,
    out_one,
    out_two,
    out_bias,
    features,
    count_one,
    bias_one,
    self_two,
    neigh_two,
    bias_two,
    cotangent,
    nbr_two,
    count_two,
    inverse_one,
    inverse_two,
    table,
    total_one,
    mean_one,
    weights_mine,
    weights_one,
    own_in,
    act_own,
    act_cols,
    counts,
    mean_send,
    mean_land,
    mean_two,
    slope_two,
    spread_send,
    spread_cols,
    direct,
    scat_send,
    scat_own,
    slope_one,
    g2_keep,
    g2_send,
    g2_core,
    g2_sum,
    g2_plane,
    g2_piece,
    g2_z,
    g2_row,
    g1_keep,
    g1_send,
    g1_core,
    g1_sum,
    g1_first_x,
    g1_part_x,
    g1_then_y,
    g1_first_y,
    g1_part_y,
    g1_then_x,
    g1_piece,
    g1_z,
    bias_mine,
    bias_core,
    bias_pair,
    bias_x,
    bias_row,
    bias_y,
    bias_chips,
    bias_z,
    send_sem,
    recv_sem,
    load_sem,
):
    b = lax.axis_index("batch")
    z = lax.axis_index("feat")
    core = b % 2
    x = (b // 2) % 4
    y = b // 8
    half = z // 4
    col = z % 4
    chip = y * 4 + x
    other = 1 - core
    sibling = {"batch": b + 1 - 2 * core, "feat": z}
    z_peers = [(z + d) % Z for d in range(1, Z)]
    ring_peers = lambda place: [(place + d) % 4 for d in range(1, 4)]
    half_peers = [(col + d) % 4 for d in range(1, 4)]
    plane_peers = [((x + d % 4) % 4, (y + d // 4) % 4) for d in range(1, 16)]

    def at_z(peer):
        return {"batch": b, "feat": peer}

    def at_plane(peer):
        return {"batch": peer[1] * 8 + peer[0] * 2 + core, "feat": z}

    used = []

    def send(src, dst, device):
        number = len(used)
        used.append(number)
        copy = pltpu.make_async_remote_copy(
            src_ref=src,
            dst_ref=dst,
            send_sem=send_sem.at[number],
            recv_sem=recv_sem.at[number],
            device_id=device,
            device_id_type=MESH,
        )
        copy.start()
        return copy

    def wait(copies):
        for copy in copies:
            copy.wait()

    def lanes(number, start=0):
        return pl.ds(pl.multiple_of(start + number * 128, 128), 128)

    def rows(number, size, start=0):
        return pl.ds(pl.multiple_of(start + number * size, 16), size)

    barrier = pltpu.get_barrier_semaphore()
    everyone = [at_z(p) for p in z_peers] + [at_plane(p) for p in plane_peers] + [sibling]
    for device in everyone:
        pl.semaphore_signal(barrier, inc=1, device_id=device, device_id_type=MESH)
    quarter = SOURCES // 4
    loads = [
        pltpu.make_async_copy(
            features_in.at[pl.ds(i * quarter, quarter), :],
            features.at[pl.ds(i * quarter, quarter), :],
            load_sem.at[i],
        )
        for i in range(4)
    ]
    pairs = (
        (self_one, weights_mine.at[pl.ds(0, COLS), :]),
        (neigh_one, weights_mine.at[pl.ds(COLS, COLS), :]),
        (count_one_in, count_one),
        (bias_one_in, bias_one),
        (self_two_in, self_two),
        (neigh_two_in, neigh_two),
        (bias_two_in, bias_two),
        (cotangent_in, cotangent),
        (nbr_two_in, nbr_two),
        (count_two_in, count_two),
    )
    loads += [
        pltpu.make_async_copy(src, dst, load_sem.at[4 + i]) for i, (src, dst) in enumerate(pairs)
    ]
    for load in loads:
        load.start()

    def widen(i, carry):
        block = pl.ds(pl.multiple_of(i * 256, 256), 256)
        table[block, :] = features[block, :].astype(F32)
        return carry

    table[pl.ds(SOURCES, 8), :] = jnp.zeros((8, COLS), F32)
    steps = quarter // 256
    loads[0].wait()
    lax.fori_loop(0, steps, widen, 0)
    own_in[pl.ds(0, OWN_SEEDS), lanes(2 * z)] = features[rows(z, OWN_SEEDS), :]
    own_in[pl.ds(OWN_SEEDS, REST), lanes(2 * z)] = features[rows(z, REST, SEEDS), :]
    for load in loads[4:]:
        load.wait()
    cols_mine = pl.ds(pl.multiple_of(core * 256, 256), 256)
    weights_one[z, rows(chip, 16), cols_mine] = weights_mine[rows(chip, 16), cols_mine]
    pl.semaphore_wait(barrier, len(everyone))

    part = weights_one.at[z, rows(chip, 16), cols_mine]
    pending_weights = [send(weights_mine.at[rows(chip, 16), cols_mine], part, at_z(p)) for p in z_peers]
    pending_own = []
    for p in z_peers:
        pending_own.append(
            send(features.at[rows(p, OWN_SEEDS), :], own_in.at[pl.ds(0, OWN_SEEDS), lanes(2 * z)], at_z(p))
        )
        pending_own.append(
            send(
                features.at[rows(p, REST, SEEDS), :],
                own_in.at[pl.ds(OWN_SEEDS, REST), lanes(2 * z)],
                at_z(p),
            )
        )

    for i in range(1, 4):
        loads[i].wait()
        lax.fori_loop(i * steps, (i + 1) * steps, widen, 0)

    for i in range(MIDDLE // 128):
        line = 1.0 / count_one[i : i + 1, :].astype(F32)
        inverse_one[i * 128 : (i + 1) * 128, :] = jnp.broadcast_to(line, (128, 128)).T

    for turn, d in enumerate((4, 3, 5, 2, 6, 1, 7, 0)):
        owner = (z + d) % Z

        def gather(g, carry, owner=owner):
            seed_base = owner * OWN_SEEDS + g * GROUP
            rest_base = SEEDS - OWN_SEEDS + owner * REST + g * GROUP
            base = jnp.where(g < OWN_SEEDS // GROUP, seed_base, rest_base)
            out = pl.multiple_of(g * GROUP, GROUP)
            for j in range(GROUP):
                terms = [table[pl.ds(index_one[base + (k * MIDDLE + j)], 1), :] for k in range(FAN_ONE)]
                total_one[pl.ds(out + j, 1), :] = tree_sum(terms)
            return carry

        lax.fori_loop(0, OWN // GROUP, gather, 0)
        seeds = total_one[pl.ds(0, OWN_SEEDS), :] * inverse_one[rows(owner, OWN_SEEDS), :]
        rest = total_one[pl.ds(OWN_SEEDS, REST), :] * inverse_one[rows(owner, REST, SEEDS), :]
        if d:
            mean_one[turn, pl.ds(0, OWN_SEEDS), :] = seeds.astype(BF16)
            mean_one[turn, pl.ds(OWN_SEEDS, REST), :] = rest.astype(BF16)
            pending_own.append(send(mean_one.at[turn], own_in.at[:, lanes(2 * z + 1)], at_z(owner)))
        else:
            own_in[pl.ds(0, OWN_SEEDS), lanes(2 * z + 1)] = seeds.astype(BF16)
            own_in[pl.ds(OWN_SEEDS, REST), lanes(2 * z + 1)] = rest.astype(BF16)
        if turn == 1:
            wait(pending_weights)
            part = weights_one.at[:, rows(chip, 16), cols_mine]
            pending_weights = [send(part, part, at_plane(p)) for p in plane_peers]
        if turn == 6:
            wait(pending_weights)
            part = weights_one.at[:, :, cols_mine]
            pending_weights = [send(part, part, sibling)]
    wait(pending_weights)
    wait(pending_own)

    def layer_one(n, carry):
        cols = pl.ds(pl.multiple_of(n * 256, 256), 256)
        pre = dot(own_in[...], weights_one[:, :, cols].reshape(2 * Z * COLS, 256)) + bias_one[:, cols]
        act_own[:, cols] = jax.nn.softplus(pre).astype(BF16)
        return carry

    lax.fori_loop(0, 2, layer_one, 0)

    pending = [
        send(act_own.at[:, lanes(p)], act_cols.at[rows(col, OWN), :], at_z(half * 4 + p)) for p in half_peers
    ]
    act_cols[rows(col, OWN), :] = act_own[:, lanes(col)]

    index_two = [
        jnp.where(count_two[...] > k, nbr_two[k : k + 1, :], -1) for k in range(FAN_TWO)
    ]
    inverse = 1.0 / count_two[...].astype(F32)
    inverse_two[...] = jnp.broadcast_to(inverse, (128, SEEDS)).T

    def count_block(i, carry):
        spot = lax.broadcasted_iota(jnp.int32, (64, SEEDS), 0) + (i % 4) * 64
        block = half * 4 + i // 4
        node = jnp.where(spot < OWN_SEEDS, block * OWN_SEEDS + spot, SEEDS - OWN_SEEDS + block * REST + spot)
        total = jnp.zeros((64, SEEDS), F32)
        for k in range(FAN_TWO):
            total = total + jnp.where(node == index_two[k], 1.0, 0.0)
        counts[rows(i, 64), :] = total.astype(BF16)
        return carry

    lax.fori_loop(0, 16, count_block, 0)
    wait(pending)

    share = dot_tn(act_cols[...], counts[...])
    mean_send[...] = (share.T * inverse_two[...]).astype(BF16)
    pending = [send(mean_send.at[rows(p, OWN_SEEDS), :], mean_land.at[z], at_z(p)) for p in z_peers]
    mean_land[z] = mean_send[rows(z, OWN_SEEDS), :]
    pre_self = dot(act_own[pl.ds(0, OWN_SEEDS), :], self_two[...]) + bias_two[...]
    wait(pending)
    for q in range(4):
        both = mean_land[q].astype(F32) + mean_land[4 + q].astype(F32)
        mean_two[:, q * 128 : (q + 1) * 128] = both.astype(BF16)

    pre_two = pre_self + dot(mean_two[...], neigh_two[...])
    slope = cotangent[...].astype(F32) * jax.nn.sigmoid(pre_two)
    slope_two[...] = slope.astype(BF16)

    spread = dot_nt(slope_two[...], neigh_two[...])
    inverse = inverse_two[rows(z, OWN_SEEDS), :]
    for q in range(4):
        cols = slice(q * 128, (q + 1) * 128)
        spread_send[:, cols] = (spread[:, cols] * inverse).astype(BF16)
    pending = [
        send(spread_send.at[:, lanes(p % 4)], spread_cols.at[rows(z, OWN_SEEDS), :], at_z(p)) for p in z_peers
    ]
    spread_cols[rows(z, OWN_SEEDS), :] = spread_send[:, lanes(col)]

    own_two = act_own[pl.ds(0, OWN_SEEDS), :]
    keep_self = jnp.where(core == 0, 1.0, 0.0).astype(BF16)
    keep_neigh = jnp.where(core == 0, 0.0, 1.0).astype(BF16)
    mixed_send = own_two * keep_neigh + mean_two[...] * keep_self
    mixed_keep = own_two * keep_self + mean_two[...] * keep_neigh
    g2_send[...] = dot_tn(mixed_send, slope_two[...]).astype(BF16)
    pending_g2 = [send(g2_send, g2_core, sibling)]
    g2_keep[...] = dot_tn(mixed_keep, slope_two[...])

    def direct_block(n, carry):
        cols = pl.ds(pl.multiple_of(n * 256, 256), 256)
        direct[:, cols] = dot_nt(slope_two[...], self_two[cols, :])
        return carry

    lax.fori_loop(0, 2, direct_block, 0)
    bias_two_sum = jnp.sum(slope_two[...].astype(F32), axis=0, keepdims=True)
    wait(pending)

    def scatter_block(i, carry):
        block = rows(i, OWN)
        scat_send[block, :] = dot(counts[block, :], spread_cols[...]).astype(BF16)
        return carry

    lax.fori_loop(0, 4, scatter_block, 0)
    pending = [
        send(scat_send.at[rows(p, OWN), :], scat_own.at[:, lanes(col)], at_z(half * 4 + p)) for p in half_peers
    ]
    scat_own[:, lanes(col)] = scat_send[rows(col, OWN), :]
    wait(pending_g2)

    def g2_pair(i, carry):
        block = rows(i, 128)
        g2_sum[block, :] = (g2_keep[block, :] + g2_core[block, :].astype(F32)).astype(BF16)
        return carry

    lax.fori_loop(0, 4, g2_pair, 0)
    pending_g2 = [
        send(g2_sum.at[rows(p[1], 128), lanes(p[0])], g2_plane.at[chip], at_plane(p)) for p in plane_peers
    ]
    g2_plane[chip] = g2_sum[rows(y, 128), lanes(x)]
    wait(pending)

    back = scat_own[pl.ds(0, OWN_SEEDS), :].astype(F32) + direct[...]
    gate = 1.0 - jnp.exp(-act_own[pl.ds(0, OWN_SEEDS), :].astype(F32))
    slope_one[pl.ds(0, OWN_SEEDS), :] = (back * gate).astype(BF16)
    back = scat_own[pl.ds(OWN_SEEDS, REST), :].astype(F32)
    gate = 1.0 - jnp.exp(-act_own[pl.ds(OWN_SEEDS, REST), :].astype(F32))
    slope_one[pl.ds(OWN_SEEDS, REST), :] = (back * gate).astype(BF16)

    def g1_block(t, carry):
        g1_send[t] = dot_tn(own_in[:, lanes(2 * t + other)], slope_one[...]).astype(BF16)
        return carry

    pending = []
    for part in range(2):
        lax.fori_loop(part * 4, part * 4 + 4, g1_block, 0)
        chunk = pl.ds(part * 4, 4)
        pending.append(send(g1_send.at[chunk], g1_core.at[chunk], sibling))

    def g1_own(t, carry):
        g1_keep[t] = dot_tn(own_in[:, lanes(2 * t + core)], slope_one[...])
        return carry

    def g1_pair(t, carry):
        both = g1_keep[t] + g1_core[t].astype(F32)
        g1_sum[t] = both.astype(BF16).reshape(4, 32, HID)
        return carry

    lax.fori_loop(0, 4, g1_own, 0)
    wait(pending[:1])
    lax.fori_loop(0, 4, g1_pair, 0)
    low, high = pl.ds(0, 4), pl.ds(4, 4)
    pending_x = [
        send(g1_sum.at[low, :, :, lanes(p)], g1_first_x.at[x], at_plane((p, y))) for p in ring_peers(x)
    ]
    g1_first_x[x] = g1_sum[0:4, :, :, lanes(x)]
    lax.fori_loop(4, 8, g1_own, 0)
    wait(pending[1:])
    lax.fori_loop(4, 8, g1_pair, 0)
    pending_y = [send(g1_sum.at[high, p], g1_first_y.at[y], at_plane((x, p))) for p in ring_peers(y)]
    g1_first_y[y] = g1_sum[4:8, y]

    bias_one_sum = jnp.sum(slope_one[...].astype(F32), axis=0, keepdims=True)
    for i in range(4):
        bias_mine[i : i + 1, :] = bias_one_sum[:, i * 128 : (i + 1) * 128]
        bias_mine[4 + i : 5 + i, :] = bias_two_sum[:, i * 128 : (i + 1) * 128]
    pending_bias = [send(bias_mine, bias_core, sibling)]

    wait(pending_g2)
    total = tree_sum([g2_plane[p].astype(F32) for p in range(16)])
    g2_piece[...] = total.astype(BF16)
    pending_g2 = [send(g2_piece.at[rows(p, 16), :], g2_z.at[z], at_z(p)) for p in z_peers]
    g2_z[z] = g2_piece[rows(z, 16), :]
    wait(pending_g2)
    total = tree_sum([g2_z[p].astype(F32) for p in range(Z)])
    g2_row[rows(z, 16), :] = total.astype(BF16)
    pending_g2 = [send(g2_row.at[rows(z, 16), :], g2_row.at[rows(z, 16), :], at_z(p)) for p in z_peers]
    wait(pending_bias)
    bias_pair[...] = bias_mine[...] + bias_core[...]
    pending_bias = [send(bias_pair, bias_x.at[x], at_plane((p, y))) for p in ring_peers(x)]
    bias_x[x] = bias_pair[...]

    wait(pending_x)

    def g1_over_x(t, carry):
        total = tree_sum([g1_first_x[p, t].astype(F32) for p in range(4)])
        g1_part_x[t] = total.astype(BF16)
        return carry

    lax.fori_loop(0, 4, g1_over_x, 0)
    pending_x = [send(g1_part_x.at[:, p], g1_then_y.at[y], at_plane((x, p))) for p in ring_peers(y)]
    g1_then_y[y] = g1_part_x[:, y]
    wait(pending_y)

    def g1_over_y(t, carry):
        total = tree_sum([g1_first_y[p, t].astype(F32) for p in range(4)])
        g1_part_y[t] = total.astype(BF16)
        return carry

    lax.fori_loop(0, 4, g1_over_y, 0)
    pending_y = [
        send(g1_part_y.at[:, :, lanes(p)], g1_then_x.at[x], at_plane((p, y))) for p in ring_peers(x)
    ]
    g1_then_x[x] = g1_part_y[:, :, lanes(x)]
    wait(pending_bias)
    bias_row[...] = tree_sum([bias_x[p] for p in range(4)])
    pending_bias = [send(bias_row, bias_y.at[y], at_plane((x, p))) for p in ring_peers(y)]
    bias_y[y] = bias_row[...]
    wait(pending_g2)
    wait(pending_x)
    wait(pending_y)

    def g1_chips(t, carry):
        g1_piece[t] = tree_sum([g1_then_y[p, t].astype(F32) for p in range(4)]).astype(BF16)
        g1_piece[4 + t] = tree_sum([g1_then_x[p, t].astype(F32) for p in range(4)]).astype(BF16)
        return carry

    lax.fori_loop(0, 4, g1_chips, 0)
    pending = [send(g1_piece.at[p], g1_z.at[z], at_z(p)) for p in z_peers]
    g1_z[z] = g1_piece[z]
    pending_g2 = [
        send(g2_row, out_two.at[core, rows(y, 128), lanes(x)], at_plane(p)) for p in plane_peers
    ]
    out_two[core, rows(y, 128), lanes(x)] = g2_row[...]
    wait(pending_bias)
    bias_chips[...] = tree_sum([bias_y[p] for p in range(4)])
    pending_bias = [send(bias_chips, bias_z.at[z], at_z(p)) for p in z_peers]
    bias_z[z] = bias_chips[...]
    wait(pending)
    total = tree_sum([g1_z[p].astype(F32) for p in range(Z)])
    out_one[core, rows(y, 32), lanes(x)] = total.astype(BF16)

    mine = out_one.at[core, rows(y, 32), lanes(x)]
    pending = [send(mine, mine, at_plane(p)) for p in plane_peers]
    wait(pending_g2)
    pending_g2 = [send(out_two.at[core], out_two.at[core], sibling)]
    wait(pending_bias)
    out_bias[...] = tree_sum([bias_z[p] for p in range(Z)])
    wait(pending)
    pending = [send(out_one.at[core], out_one.at[core], sibling)]
    wait(pending_g2)
    wait(pending)
    assert len(used) <= N_COPIES


def training_step(*operands):
    bf16 = [
        (SOURCES, COLS),
        jnp.int32,
        None,
        (HID, HID),
        (HID, HID),
        None,
        (OWN_SEEDS, HID),
        jnp.int32,
        jnp.int32,
        None,
        None,
        None,
        None,
        (Z - 1, OWN, COLS),
        (2 * COLS, HID),
        (Z, 2 * COLS, HID),
        (OWN, 2 * Z * COLS),
        (OWN, HID),
        (4 * OWN, 128),
        (4 * OWN, SEEDS),
        (SEEDS, 128),
        (Z, OWN_SEEDS, 128),
        (OWN_SEEDS, HID),
        (OWN_SEEDS, HID),
        (OWN_SEEDS, HID),
        (SEEDS, 128),
        None,
        (4 * OWN, 128),
        (OWN, HID),
        (OWN, HID),
        None,
        (HID, HID),
        (HID, HID),
        (HID, HID),
        (16, 128, 128),
        (128, 128),
        (Z, 16, 128),
        (128, 128),
        None,
        (Z, 128, HID),
        (Z, 128, HID),
        (Z, 4, 32, HID),
        (4, 4, 4, 32, 128),
        (4, 4, 32, 128),
        (4, 4, 32, 128),
        (4, 4, 32, HID),
        (4, 32, HID),
        (4, 4, 32, 128),
        (Z, 32, 128),
        (Z, 32, 128),
    ]
    wide = iter(
        [
            (1, HID),
            (1, HID),
            (MIDDLE, 128),
            (SEEDS, 128),
            (SOURCES + 8, COLS),
            (OWN, COLS),
            (OWN_SEEDS, HID),
            (HID, HID),
            (Z, 128, HID),
        ]
    )
    whole = iter([(16, 128), (FAN_TWO, SEEDS), (1, SEEDS)])
    scratch = []
    for entry in bf16:
        if entry is None:
            scratch.append(pltpu.VMEM(next(wide), F32))
        elif entry is jnp.int32:
            scratch.append(pltpu.VMEM(next(whole), jnp.int32))
        else:
            scratch.append(pltpu.VMEM(entry, BF16))
    tile = (8, 128)
    four = (4, *tile)
    scratch += [pltpu.VMEM(s, F32) for s in (tile, tile, tile, four, tile, four, tile, (Z, *tile))]
    scratch += [pltpu.SemaphoreType.DMA((N_COPIES,)), pltpu.SemaphoreType.DMA((N_COPIES,))]
    scratch += [pltpu.SemaphoreType.DMA((14,))]
    return pl.pallas_call(
        step_kernel,
        name="training_step",
        out_shape=(
            jax.ShapeDtypeStruct((2, 128, HID), BF16),
            jax.ShapeDtypeStruct((2, HID, HID), BF16),
            jax.ShapeDtypeStruct(tile, F32),
        ),
        in_specs=[SMEM] + [HBM] * (len(operands) - 1),
        out_specs=(VMEM, VMEM, VMEM),
        scratch_shapes=scratch,
        compiler_params=pltpu.CompilerParams(
            collective_id=0, has_side_effects=True, vmem_limit_bytes=60 << 20
        ),
    )(*operands)


def on_device(
    features,
    nbr_one,
    count_one,
    nbr_two,
    count_two,
    self_one,
    neigh_one,
    bias_one,
    self_two,
    neigh_two,
    bias_two,
    cotangent,
):
    slot = lax.broadcasted_iota(jnp.int32, nbr_one.shape, 0)
    index_one = jnp.where(slot < count_one[None, :], nbr_one, SOURCES).reshape(-1)
    one, two, bias = training_step(
        index_one,
        features,
        count_one.reshape(MIDDLE // 128, 128),
        self_one,
        neigh_one,
        bias_one[None, :],
        self_two,
        neigh_two,
        bias_two[None, :],
        cotangent,
        nbr_two,
        count_two[None, :],
    )
    one, two = one.astype(F32), two.astype(F32)
    return one[0], one[1], bias[:4].reshape(HID), two[0], two[1], bias[4:].reshape(HID)


def solution(mesh):
    in_specs = (
        P("batch", "feat"),
        P(None, "batch"),
        P("batch"),
        P(None, "batch"),
        P("batch"),
        P("feat", None),
        P("feat", None),
        P(),
        P(),
        P(),
        P(),
        P(("batch", "feat"), None),
    )
    out_specs = (P("feat", None), P("feat", None), P(), P(), P(), P())
    return jax.shard_map(
        on_device, mesh=mesh, in_specs=in_specs, out_specs=out_specs, check_vma=False
    )
```

```python
import functools

import jax
import jax.numpy as jnp
from jax import lax
from jax.experimental import pallas as pl
from jax.experimental.pallas import tpu as pltpu
from jax.sharding import PartitionSpec as P

MESH = pl.DeviceIdType.MESH
F32 = jnp.float32
BF16 = jnp.bfloat16
VMEM = pl.BlockSpec(memory_space=pltpu.VMEM)
HBM = pl.BlockSpec(memory_space=pltpu.HBM)

SOURCES = 8192
MIDDLE = 2048
SEEDS = 512
HID = 512
COLS = 128
FAN_ONE = 15
FAN_TWO = 10
Z = 8
OWN = 256
OWN_SEEDS = 64
REST = 192
GROUP = 32


def tree_sum(terms):
    while len(terms) > 1:
        odd = [terms[-1]] if len(terms) % 2 else []
        terms = [a + b for a, b in zip(terms[::2], terms[1::2])] + odd
    return terms[0]


def dot(a, b):
    return jnp.dot(a, b, preferred_element_type=F32)


def dot_tn(a, b):
    return lax.dot_general(a, b, (((0,), (0,)), ((), ())), preferred_element_type=F32)


def dot_nt(a, b):
    return lax.dot_general(a, b, (((1,), (1,)), ((), ())), preferred_element_type=F32)


N_COPIES = 200


def step_kernel(
    index_one_in,
    features_in,
    count_one_in,
    self_one,
    neigh_one,
    bias_one_in,
    self_two_in,
    neigh_two_in,
    bias_two_in,
    cotangent_in,
    nbr_two_in,
    count_two_in,
    result_self_one,
    result_neigh_one,
    result_self_two,
    result_neigh_two,
    result_bias_one,
    result_bias_two,
    index_one,
    out_one,
    out_two,
    own_in_t,
    features,
    count_one,
    bias_one,
    self_two,
    neigh_two,
    bias_two,
    cotangent,
    nbr_two,
    count_two,
    inverse_one,
    inverse_two,
    table,
    total_one,
    mean_one,
    weights_mine,
    weights_one,
    own_in,
    act_own,
    act_cols,
    counts,
    mean_send,
    mean_land,
    mean_two,
    slope_two,
    spread_send,
    spread_cols,
    direct,
    scat_send,
    scat_own,
    slope_one,
    g2_keep,
    g2_send,
    g2_core,
    g2_sum,
    g2_plane,
    g2_piece,
    g2_z,
    g2_row,
    g1_keep,
    g1_send,
    g1_core,
    g1_sum,
    g1_first_x,
    g1_part_x,
    g1_then_y,
    g1_first_y,
    g1_part_y,
    g1_then_x,
    g1_piece,
    g1_z,
    bias_mine,
    bias_core,
    bias_pair,
    bias_x,
    bias_row,
    bias_y,
    bias_chips,
    bias_z,
    send_sem,
    recv_sem,
    load_sem,
):
    b = lax.axis_index("batch")
    z = lax.axis_index("feat")
    core = b % 2
    x = (b // 2) % 4
    y = b // 8
    half = z // 4
    col = z % 4
    chip = y * 4 + x
    other = 1 - core
    sibling = {"batch": b + 1 - 2 * core, "feat": z}
    z_peers = [(z + d) % Z for d in range(1, Z)]
    ring_peers = lambda place: [(place + d) % 4 for d in range(1, 4)]
    half_peers = [(col + d) % 4 for d in range(1, 4)]
    plane_peers = [((x + d % 4) % 4, (y + d // 4) % 4) for d in range(1, 16)]

    def at_z(peer):
        return {"batch": b, "feat": peer}

    def at_plane(peer):
        return {"batch": peer[1] * 8 + peer[0] * 2 + core, "feat": z}

    used = []

    def send(src, dst, device):
        number = len(used)
        used.append(number)
        copy = pltpu.make_async_remote_copy(
            src_ref=src,
            dst_ref=dst,
            send_sem=send_sem.at[number],
            recv_sem=recv_sem.at[number],
            device_id=device,
            device_id_type=MESH,
        )
        copy.start()
        return copy

    def wait(copies):
        for copy in copies:
            copy.wait()

    def lanes(number, start=0):
        return pl.ds(pl.multiple_of(start + number * 128, 128), 128)

    def rows(number, size, start=0):
        return pl.ds(pl.multiple_of(start + number * size, 16), size)

    barrier = pltpu.get_barrier_semaphore()
    everyone = [at_z(p) for p in z_peers] + [at_plane(p) for p in plane_peers] + [sibling]
    for device in everyone:
        pl.semaphore_signal(barrier, inc=1, device_id=device, device_id_type=MESH)
    quarter = SOURCES // 4
    loads = [
        pltpu.make_async_copy(
            features_in.at[pl.ds(i * quarter, quarter), :],
            features.at[pl.ds(i * quarter, quarter), :],
            load_sem.at[i],
        )
        for i in range(4)
    ]
    pairs = (
        (self_one, weights_mine.at[pl.ds(0, COLS), :]),
        (neigh_one, weights_mine.at[pl.ds(COLS, COLS), :]),
        (count_one_in, count_one),
        (bias_one_in, bias_one),
        (self_two_in, self_two),
        (neigh_two_in, neigh_two),
        (bias_two_in, bias_two),
        (cotangent_in, cotangent),
        (nbr_two_in, nbr_two),
        (count_two_in, count_two),
        (index_one_in, index_one),
    )
    loads += [
        pltpu.make_async_copy(src, dst, load_sem.at[4 + i]) for i, (src, dst) in enumerate(pairs)
    ]
    for load in loads:
        load.start()

    def widen(i, carry):
        block = pl.ds(pl.multiple_of(i * 256, 256), 256)
        table[block, :] = features[block, :].astype(F32)
        return carry

    table[pl.ds(SOURCES, 8), :] = jnp.zeros((8, COLS), F32)
    steps = quarter // 256
    for i in range(4):
        loads[i].wait()
        lax.fori_loop(i * steps, (i + 1) * steps, widen, 0)
    own_in[pl.ds(0, OWN_SEEDS), lanes(2 * z)] = features[rows(z, OWN_SEEDS), :]
    own_in[pl.ds(OWN_SEEDS, REST), lanes(2 * z)] = features[rows(z, REST, SEEDS), :]
    for load in loads[4:]:
        load.wait()

    for i in range(MIDDLE // 128):
        line = 1.0 / count_one[i : i + 1, :].astype(F32)
        inverse_one[i * 128 : (i + 1) * 128, :] = jnp.broadcast_to(line, (128, 128)).T

    cols_mine = pl.ds(pl.multiple_of(core * 256, 256), 256)
    weights_one[z, rows(chip, 16), cols_mine] = weights_mine[rows(chip, 16), cols_mine]
    pl.semaphore_wait(barrier, len(everyone))

    part = weights_one.at[z, rows(chip, 16), cols_mine]
    pending_weights = [send(weights_mine.at[rows(chip, 16), cols_mine], part, at_z(p)) for p in z_peers]
    pending_own = []
    for p in z_peers:
        pending_own.append(
            send(features.at[rows(p, OWN_SEEDS), :], own_in.at[pl.ds(0, OWN_SEEDS), lanes(2 * z)], at_z(p))
        )
        pending_own.append(
            send(
                features.at[rows(p, REST, SEEDS), :],
                own_in.at[pl.ds(OWN_SEEDS, REST), lanes(2 * z)],
                at_z(p),
            )
        )

    for turn, d in enumerate((4, 3, 5, 2, 6, 1, 7, 0)):
        owner = (z + d) % Z

        def gather(g, carry, owner=owner):
            seed_base = owner * OWN_SEEDS + g * GROUP
            rest_base = SEEDS - OWN_SEEDS + owner * REST + g * GROUP
            base = jnp.where(g < OWN_SEEDS // GROUP, seed_base, rest_base)
            out = pl.multiple_of(g * GROUP, GROUP)
            for j in range(GROUP):
                terms = [table[pl.ds(index_one[base + (k * MIDDLE + j)], 1), :] for k in range(FAN_ONE)]
                total_one[pl.ds(out + j, 1), :] = tree_sum(terms)
            return carry

        lax.fori_loop(0, OWN // GROUP, gather, 0)
        seeds = total_one[pl.ds(0, OWN_SEEDS), :] * inverse_one[rows(owner, OWN_SEEDS), :]
        rest = total_one[pl.ds(OWN_SEEDS, REST), :] * inverse_one[rows(owner, REST, SEEDS), :]
        if d:
            mean_one[turn, pl.ds(0, OWN_SEEDS), :] = seeds.astype(BF16)
            mean_one[turn, pl.ds(OWN_SEEDS, REST), :] = rest.astype(BF16)
            pending_own.append(send(mean_one.at[turn], own_in.at[:, lanes(2 * z + 1)], at_z(owner)))
        else:
            own_in[pl.ds(0, OWN_SEEDS), lanes(2 * z + 1)] = seeds.astype(BF16)
            own_in[pl.ds(OWN_SEEDS, REST), lanes(2 * z + 1)] = rest.astype(BF16)
        if turn == 1:
            wait(pending_weights)
            part = weights_one.at[:, rows(chip, 16), cols_mine]
            pending_weights = [send(part, part, at_plane(p)) for p in plane_peers]
        if turn == 6:
            wait(pending_weights)
            part = weights_one.at[:, :, cols_mine]
            pending_weights = [send(part, part, sibling)]
    wait(pending_weights)
    wait(pending_own)

    def layer_one(d, carry):
        cols = lanes((col + d) % 4)
        pre = dot(own_in[...], weights_one[:, :, cols].reshape(2 * Z * COLS, 128)) + bias_one[:, cols]
        act_own[:, cols] = jax.nn.softplus(pre).astype(BF16)
        return carry

    pending = []
    for d in (2, 1, 3):
        lax.fori_loop(d, d + 1, layer_one, 0)
        p = (col + d) % 4
        pending.append(send(act_own.at[:, lanes(p)], act_cols.at[rows(col, OWN), :], at_z(half * 4 + p)))
    lax.fori_loop(0, 1, layer_one, 0)
    act_cols[rows(col, OWN), :] = act_own[:, lanes(col)]

    index_two = [
        jnp.where(count_two[...] > k, nbr_two[k : k + 1, :], -1) for k in range(FAN_TWO)
    ]
    inverse = 1.0 / count_two[...].astype(F32)
    inverse_two[...] = jnp.broadcast_to(inverse, (128, SEEDS)).T

    def count_block(i, carry):
        spot = lax.broadcasted_iota(jnp.int32, (64, SEEDS), 0) + (i % 4) * 64
        block = half * 4 + i // 4
        node = jnp.where(spot < OWN_SEEDS, block * OWN_SEEDS + spot, SEEDS - OWN_SEEDS + block * REST + spot)
        total = jnp.zeros((64, SEEDS), F32)
        for k in range(FAN_TWO):
            total = total + jnp.where(node == index_two[k], 1.0, 0.0)
        counts[rows(i, 64), :] = total.astype(BF16)
        return carry

    lax.fori_loop(0, 16, count_block, 0)
    wait(pending)

    share = dot_tn(act_cols[...], counts[...])
    mean_send[...] = (share.T * inverse_two[...]).astype(BF16)
    pending = [send(mean_send.at[rows(p, OWN_SEEDS), :], mean_land.at[z], at_z(p)) for p in z_peers]
    mean_land[z] = mean_send[rows(z, OWN_SEEDS), :]
    pre_self = dot(act_own[pl.ds(0, OWN_SEEDS), :], self_two[...]) + bias_two[...]

    def turn_block(t, carry):
        own_in_t[rows(t, 128), :] = own_in[:, lanes(t)].T
        return carry

    lax.fori_loop(0, 2 * Z, turn_block, 0)
    wait(pending)
    for q in range(4):
        both = mean_land[q].astype(F32) + mean_land[4 + q].astype(F32)
        mean_two[:, q * 128 : (q + 1) * 128] = both.astype(BF16)

    pre_two = pre_self + dot(mean_two[...], neigh_two[...])
    slope = cotangent[...].astype(F32) * jax.nn.sigmoid(pre_two)
    slope_two[...] = slope.astype(BF16)

    spread = dot_nt(slope_two[...], neigh_two[...])
    inverse = inverse_two[rows(z, OWN_SEEDS), :]
    for q in range(4):
        cols = slice(q * 128, (q + 1) * 128)
        spread_send[:, cols] = (spread[:, cols] * inverse).astype(BF16)
    pending = [
        send(spread_send.at[:, lanes(p % 4)], spread_cols.at[rows(z, OWN_SEEDS), :], at_z(p)) for p in z_peers
    ]
    spread_cols[rows(z, OWN_SEEDS), :] = spread_send[:, lanes(col)]

    own_two = act_own[pl.ds(0, OWN_SEEDS), :]
    keep_self = jnp.where(core == 0, 1.0, 0.0).astype(BF16)
    keep_neigh = jnp.where(core == 0, 0.0, 1.0).astype(BF16)
    mixed_send = own_two * keep_neigh + mean_two[...] * keep_self
    mixed_keep = own_two * keep_self + mean_two[...] * keep_neigh
    g2_send[...] = dot_tn(mixed_send, slope_two[...]).astype(BF16)
    pending_g2 = [send(g2_send, g2_core, sibling)]
    g2_keep[...] = dot_tn(mixed_keep, slope_two[...])

    def direct_block(n, carry):
        cols = pl.ds(pl.multiple_of(n * 256, 256), 256)
        direct[:, cols] = dot_nt(slope_two[...], self_two[cols, :])
        return carry

    lax.fori_loop(0, 2, direct_block, 0)
    bias_two_sum = jnp.sum(slope_two[...].astype(F32), axis=0, keepdims=True)
    wait(pending)

    def scatter_block(d, carry):
        block = rows((col + d) % 4, OWN)
        scat_send[block, :] = dot(counts[block, :], spread_cols[...]).astype(BF16)
        return carry

    pending = []
    for first in (2, 0):
        lax.fori_loop(first, first + 2, scatter_block, 0)
        for d in (2, 3) if first else (1,):
            p = (col + d) % 4
            part = scat_send.at[rows(p, OWN), :]
            pending.append(send(part, scat_own.at[:, lanes(col)], at_z(half * 4 + p)))
    scat_own[:, lanes(col)] = scat_send[rows(col, OWN), :]
    wait(pending_g2)

    def g2_pair(i, carry):
        block = rows(i, 128)
        g2_sum[block, :] = (g2_keep[block, :] + g2_core[block, :].astype(F32)).astype(BF16)
        return carry

    lax.fori_loop(0, 4, g2_pair, 0)
    pending_g2 = [
        send(g2_sum.at[rows(p[1], 128), lanes(p[0])], g2_plane.at[chip], at_plane(p)) for p in plane_peers
    ]
    g2_plane[chip] = g2_sum[rows(y, 128), lanes(x)]
    wait(pending)

    back = scat_own[pl.ds(0, OWN_SEEDS), :].astype(F32) + direct[...]
    gate = 1.0 - jnp.exp(-act_own[pl.ds(0, OWN_SEEDS), :].astype(F32))
    slope_one[pl.ds(0, OWN_SEEDS), :] = (back * gate).astype(BF16)
    back = scat_own[pl.ds(OWN_SEEDS, REST), :].astype(F32)
    gate = 1.0 - jnp.exp(-act_own[pl.ds(OWN_SEEDS, REST), :].astype(F32))
    slope_one[pl.ds(OWN_SEEDS, REST), :] = (back * gate).astype(BF16)

    def g1_block(t, carry):
        g1_send[t] = dot(own_in_t[rows(2 * t + other, 128), :], slope_one[...]).astype(BF16)
        return carry

    pending = []
    for part in range(2):
        lax.fori_loop(part * 4, part * 4 + 4, g1_block, 0)
        chunk = pl.ds(part * 4, 4)
        pending.append(send(g1_send.at[chunk], g1_core.at[chunk], sibling))

    def g1_own(t, carry):
        g1_keep[t] = dot(own_in_t[rows(2 * t + core, 128), :], slope_one[...])
        return carry

    def g1_pair(t, carry):
        both = g1_keep[t] + g1_core[t].astype(F32)
        g1_sum[t] = both.astype(BF16).reshape(4, 32, HID)
        return carry

    lax.fori_loop(0, 4, g1_own, 0)
    wait(pending[:1])
    lax.fori_loop(0, 4, g1_pair, 0)
    low, high = pl.ds(0, 4), pl.ds(4, 4)
    pending_x = [
        send(g1_sum.at[low, :, :, lanes(p)], g1_first_x.at[x], at_plane((p, y))) for p in ring_peers(x)
    ]
    g1_first_x[x] = g1_sum[0:4, :, :, lanes(x)]
    lax.fori_loop(4, 8, g1_own, 0)
    wait(pending[1:])
    lax.fori_loop(4, 8, g1_pair, 0)
    pending_y = [send(g1_sum.at[high, p], g1_first_y.at[y], at_plane((x, p))) for p in ring_peers(y)]
    g1_first_y[y] = g1_sum[4:8, y]

    bias_one_sum = jnp.sum(slope_one[...].astype(F32), axis=0, keepdims=True)
    for i in range(4):
        bias_mine[i : i + 1, :] = bias_one_sum[:, i * 128 : (i + 1) * 128]
        bias_mine[4 + i : 5 + i, :] = bias_two_sum[:, i * 128 : (i + 1) * 128]
    pending_bias = [send(bias_mine, bias_core, sibling)]

    wait(pending_g2)
    total = tree_sum([g2_plane[p].astype(F32) for p in range(16)])
    g2_piece[...] = total.astype(BF16)
    pending_g2 = [send(g2_piece.at[rows(p, 16), :], g2_z.at[z], at_z(p)) for p in z_peers]
    g2_z[z] = g2_piece[rows(z, 16), :]
    wait(pending_g2)
    total = tree_sum([g2_z[p].astype(F32) for p in range(Z)])
    g2_row[rows(z, 16), :] = total.astype(BF16)
    pending_g2 = [send(g2_row.at[rows(z, 16), :], g2_row.at[rows(z, 16), :], at_z(p)) for p in z_peers]
    wait(pending_bias)
    bias_pair[...] = bias_mine[...] + bias_core[...]
    pending_bias = [send(bias_pair, bias_x.at[x], at_plane((p, y))) for p in ring_peers(x)]
    bias_x[x] = bias_pair[...]

    wait(pending_x)

    def g1_over_x(t, carry):
        total = tree_sum([g1_first_x[p, t].astype(F32) for p in range(4)])
        g1_part_x[t] = total.astype(BF16)
        return carry

    lax.fori_loop(0, 4, g1_over_x, 0)
    pending_x = [send(g1_part_x.at[:, p], g1_then_y.at[y], at_plane((x, p))) for p in ring_peers(y)]
    g1_then_y[y] = g1_part_x[:, y]
    wait(pending_y)

    def g1_over_y(t, carry):
        total = tree_sum([g1_first_y[p, t].astype(F32) for p in range(4)])
        g1_part_y[t] = total.astype(BF16)
        return carry

    lax.fori_loop(0, 4, g1_over_y, 0)
    pending_y = [
        send(g1_part_y.at[:, :, lanes(p)], g1_then_x.at[x], at_plane((p, y))) for p in ring_peers(x)
    ]
    g1_then_x[x] = g1_part_y[:, :, lanes(x)]
    wait(pending_bias)
    bias_row[...] = tree_sum([bias_x[p] for p in range(4)])
    pending_bias = [send(bias_row, bias_y.at[y], at_plane((x, p))) for p in ring_peers(y)]
    bias_y[y] = bias_row[...]
    wait(pending_g2)
    wait(pending_x)
    wait(pending_y)

    def g1_chips(t, carry):
        g1_piece[t] = tree_sum([g1_then_y[p, t].astype(F32) for p in range(4)]).astype(BF16)
        g1_piece[4 + t] = tree_sum([g1_then_x[p, t].astype(F32) for p in range(4)]).astype(BF16)
        return carry

    lax.fori_loop(0, 4, g1_chips, 0)
    pending = [send(g1_piece.at[p], g1_z.at[z], at_z(p)) for p in z_peers]
    g1_z[z] = g1_piece[z]
    pending_g2 = [
        send(g2_row, out_two.at[core, rows(y, 128), lanes(x)], at_plane(p)) for p in plane_peers
    ]
    out_two[core, rows(y, 128), lanes(x)] = g2_row[...]
    wait(pending_bias)
    bias_chips[...] = tree_sum([bias_y[p] for p in range(4)])
    pending_bias = [send(bias_chips, bias_z.at[z], at_z(p)) for p in z_peers]
    bias_z[z] = bias_chips[...]
    wait(pending)
    total = tree_sum([g1_z[p].astype(F32) for p in range(Z)])
    out_one[core, rows(y, 32), lanes(x)] = total.astype(BF16)

    mine = out_one.at[core, rows(y, 32), lanes(x)]
    pending = [send(mine, mine, at_plane(p)) for p in plane_peers]
    wait(pending_g2)
    pending_g2 = [send(out_two.at[core], out_two.at[core], sibling)]
    wait(pending_bias)
    total = tree_sum([bias_z[p] for p in range(Z)])
    for i in range(4):
        result_bias_one[:, i * 128 : (i + 1) * 128] = total[i : i + 1, :]
        result_bias_two[:, i * 128 : (i + 1) * 128] = total[4 + i : 5 + i, :]
    wait(pending)
    pending = [send(out_one.at[core], out_one.at[core], sibling)]
    wait(pending_g2)
    stores = [
        pltpu.make_async_copy(out_two.at[0], result_self_two, load_sem.at[0]),
        pltpu.make_async_copy(out_two.at[1], result_neigh_two, load_sem.at[1]),
        pltpu.make_async_copy(out_one.at[0], result_self_one, load_sem.at[2]),
        pltpu.make_async_copy(out_one.at[1], result_neigh_one, load_sem.at[3]),
    ]
    stores[0].start()
    stores[1].start()
    wait(pending)
    stores[2].start()
    stores[3].start()
    for store in stores:
        store.wait()
    assert len(used) <= N_COPIES


def training_step(*operands):
    bf16 = [
        (2, 128, HID),
        (2, HID, HID),
        (2 * Z * COLS, OWN),
        (SOURCES, COLS),
        jnp.int32,
        None,
        (HID, HID),
        (HID, HID),
        None,
        (OWN_SEEDS, HID),
        jnp.int32,
        jnp.int32,
        None,
        None,
        None,
        None,
        (Z - 1, OWN, COLS),
        (2 * COLS, HID),
        (Z, 2 * COLS, HID),
        (OWN, 2 * Z * COLS),
        (OWN, HID),
        (4 * OWN, 128),
        (4 * OWN, SEEDS),
        (SEEDS, 128),
        (Z, OWN_SEEDS, 128),
        (OWN_SEEDS, HID),
        (OWN_SEEDS, HID),
        (OWN_SEEDS, HID),
        (SEEDS, 128),
        None,
        (4 * OWN, 128),
        (OWN, HID),
        (OWN, HID),
        None,
        (HID, HID),
        (HID, HID),
        (HID, HID),
        (16, 128, 128),
        (128, 128),
        (Z, 16, 128),
        (128, 128),
        None,
        (Z, 128, HID),
        (Z, 128, HID),
        (Z, 4, 32, HID),
        (4, 4, 4, 32, 128),
        (4, 4, 32, 128),
        (4, 4, 32, 128),
        (4, 4, 32, HID),
        (4, 32, HID),
        (4, 4, 32, 128),
        (Z, 32, 128),
        (Z, 32, 128),
    ]
    wide = iter(
        [
            (1, HID),
            (1, HID),
            (MIDDLE, 128),
            (SEEDS, 128),
            (SOURCES + 8, COLS),
            (OWN, COLS),
            (OWN_SEEDS, HID),
            (HID, HID),
            (Z, 128, HID),
        ]
    )
    whole = iter([(16, 128), (FAN_TWO, SEEDS), (1, SEEDS)])
    scratch = [pltpu.SMEM((FAN_ONE * MIDDLE,), jnp.int32)]
    for entry in bf16:
        if entry is None:
            scratch.append(pltpu.VMEM(next(wide), F32))
        elif entry is jnp.int32:
            scratch.append(pltpu.VMEM(next(whole), jnp.int32))
        else:
            scratch.append(pltpu.VMEM(entry, BF16))
    tile = (8, 128)
    four = (4, *tile)
    scratch += [pltpu.VMEM(s, F32) for s in (tile, tile, tile, four, tile, four, tile, (Z, *tile))]
    scratch += [pltpu.SemaphoreType.DMA((N_COPIES,)), pltpu.SemaphoreType.DMA((N_COPIES,))]
    scratch += [pltpu.SemaphoreType.DMA((15,))]
    return pl.pallas_call(
        step_kernel,
        name="training_step",
        out_shape=(
            jax.ShapeDtypeStruct((128, HID), BF16),
            jax.ShapeDtypeStruct((128, HID), BF16),
            jax.ShapeDtypeStruct((HID, HID), BF16),
            jax.ShapeDtypeStruct((HID, HID), BF16),
            jax.ShapeDtypeStruct((1, HID), F32),
            jax.ShapeDtypeStruct((1, HID), F32),
        ),
        in_specs=[HBM] * len(operands),
        out_specs=(HBM, HBM, HBM, HBM, VMEM, VMEM),
        scratch_shapes=scratch,
        compiler_params=pltpu.CompilerParams(
            collective_id=0, has_side_effects=True, vmem_limit_bytes=60 << 20
        ),
    )(*operands)


def widen_kernel(*refs):
    half = len(refs) // 2
    for narrow, wide in zip(refs[:half], refs[half:]):
        wide[...] = narrow[...].astype(F32)


def widen_all(*arrays):
    steps = 2
    specs = [
        pl.BlockSpec((a.shape[0] // steps, HID), lambda i: (i, 0))
        if a.shape[0] > 1
        else pl.BlockSpec((1, HID), lambda i: (0, 0))
        for a in arrays
    ]
    return pl.pallas_call(
        widen_kernel,
        name="widen",
        grid=(steps,),
        out_shape=[jax.ShapeDtypeStruct(a.shape, F32) for a in arrays],
        in_specs=specs,
        out_specs=specs,
        compiler_params=pltpu.CompilerParams(vmem_limit_bytes=60 << 20),
    )(*arrays)


def on_device(
    features,
    nbr_one,
    count_one,
    nbr_two,
    count_two,
    self_one,
    neigh_one,
    bias_one,
    self_two,
    neigh_two,
    bias_two,
    cotangent,
):
    slot = lax.broadcasted_iota(jnp.int32, nbr_one.shape, 0)
    index_one = jnp.where(slot < count_one[None, :], nbr_one, SOURCES).reshape(-1)
    sums = training_step(
        index_one,
        features,
        count_one.reshape(MIDDLE // 128, 128),
        self_one,
        neigh_one,
        bias_one[None, :],
        self_two,
        neigh_two,
        bias_two[None, :],
        cotangent,
        nbr_two,
        count_two[None, :],
    )
    g_self_one, g_neigh_one, g_self_two, g_neigh_two, g_bias_one, g_bias_two = widen_all(*sums)
    return (
        g_self_one,
        g_neigh_one,
        g_bias_one.reshape(HID),
        g_self_two,
        g_neigh_two,
        g_bias_two.reshape(HID),
    )


def solution(mesh):
    in_specs = (
        P("batch", "feat"),
        P(None, "batch"),
        P("batch"),
        P(None, "batch"),
        P("batch"),
        P("feat", None),
        P("feat", None),
        P(),
        P(),
        P(),
        P(),
        P(("batch", "feat"), None),
    )
    out_specs = (P("feat", None), P("feat", None), P(), P(), P(), P())
    return jax.shard_map(
        on_device, mesh=mesh, in_specs=in_specs, out_specs=out_specs, check_vma=False
    )
```

```python
import functools

import jax
import jax.numpy as jnp
from jax import lax
from jax.experimental import pallas as pl
from jax.experimental.pallas import tpu as pltpu
from jax.sharding import PartitionSpec as P

MESH = pl.DeviceIdType.MESH
F32 = jnp.float32
BF16 = jnp.bfloat16
VMEM = pl.BlockSpec(memory_space=pltpu.VMEM)
HBM = pl.BlockSpec(memory_space=pltpu.HBM)

SOURCES = 8192
MIDDLE = 2048
SEEDS = 512
HID = 512
COLS = 128
FAN_ONE = 15
FAN_TWO = 10
Z = 8
OWN = 256
OWN_SEEDS = 64
REST = 192
GROUP = 32


def tree_sum(terms):
    while len(terms) > 1:
        odd = [terms[-1]] if len(terms) % 2 else []
        terms = [a + b for a, b in zip(terms[::2], terms[1::2])] + odd
    return terms[0]


def dot(a, b):
    return jnp.dot(a, b, preferred_element_type=F32)


def dot_tn(a, b):
    return lax.dot_general(a, b, (((0,), (0,)), ((), ())), preferred_element_type=F32)


def dot_nt(a, b):
    return lax.dot_general(a, b, (((1,), (1,)), ((), ())), preferred_element_type=F32)


N_COPIES = 200


def step_kernel(
    nbr_one_in,
    features_in,
    count_one_in,
    self_one,
    neigh_one,
    bias_one_in,
    self_two_in,
    neigh_two_in,
    bias_two_in,
    cotangent_in,
    nbr_two_in,
    count_two_in,
    result_self_one,
    result_neigh_one,
    result_self_two,
    result_neigh_two,
    result_bias_one,
    result_bias_two,
    index_one,
    masked,
    nbr_one,
    out_one,
    out_two,
    own_in_t,
    features,
    count_one,
    bias_one,
    self_two,
    neigh_two,
    bias_two,
    cotangent,
    nbr_two,
    count_two,
    inverse_one,
    inverse_two,
    table,
    total_one,
    mean_one,
    weights_mine,
    weights_one,
    own_in,
    act_own,
    act_cols,
    counts,
    mean_send,
    mean_land,
    mean_two,
    slope_two,
    spread_send,
    spread_cols,
    direct,
    scat_send,
    scat_own,
    slope_one,
    g2_keep,
    g2_send,
    g2_core,
    g2_sum,
    g2_plane,
    g2_piece,
    g2_z,
    g2_row,
    g1_keep,
    g1_send,
    g1_core,
    g1_sum,
    g1_first_x,
    g1_part_x,
    g1_then_y,
    g1_first_y,
    g1_part_y,
    g1_then_x,
    g1_piece,
    g1_z,
    bias_mine,
    bias_core,
    bias_pair,
    bias_x,
    bias_row,
    bias_y,
    bias_chips,
    bias_z,
    send_sem,
    recv_sem,
    load_sem,
):
    b = lax.axis_index("batch")
    z = lax.axis_index("feat")
    core = b % 2
    x = (b // 2) % 4
    y = b // 8
    half = z // 4
    col = z % 4
    chip = y * 4 + x
    other = 1 - core
    sibling = {"batch": b + 1 - 2 * core, "feat": z}
    z_peers = [(z + d) % Z for d in (4, 3, 5, 2, 6, 1, 7)]
    ring_peers = lambda place: [(place + d) % 4 for d in range(1, 4)]
    half_peers = [(col + d) % 4 for d in range(1, 4)]
    plane_peers = [((x + d % 4) % 4, (y + d // 4) % 4) for d in range(1, 16)]

    def at_z(peer):
        return {"batch": b, "feat": peer}

    def at_plane(peer):
        return {"batch": peer[1] * 8 + peer[0] * 2 + core, "feat": z}

    used = []

    def send(src, dst, device):
        number = len(used)
        used.append(number)
        copy = pltpu.make_async_remote_copy(
            src_ref=src,
            dst_ref=dst,
            send_sem=send_sem.at[number],
            recv_sem=recv_sem.at[number],
            device_id=device,
            device_id_type=MESH,
        )
        copy.start()
        return copy

    def wait(copies):
        for copy in copies:
            copy.wait()

    def lanes(number, start=0):
        return pl.ds(pl.multiple_of(start + number * 128, 128), 128)

    def rows(number, size, start=0):
        return pl.ds(pl.multiple_of(start + number * size, 16), size)

    barrier = pltpu.get_barrier_semaphore()
    everyone = [at_z(p) for p in z_peers] + [at_plane(p) for p in plane_peers] + [sibling]
    for device in everyone:
        pl.semaphore_signal(barrier, inc=1, device_id=device, device_id_type=MESH)
    quarter = SOURCES // 4
    loads = [
        pltpu.make_async_copy(
            features_in.at[pl.ds(i * quarter, quarter), :],
            features.at[pl.ds(i * quarter, quarter), :],
            load_sem.at[i],
        )
        for i in range(4)
    ]
    pairs = (
        (self_one, weights_mine.at[pl.ds(0, COLS), :]),
        (neigh_one, weights_mine.at[pl.ds(COLS, COLS), :]),
        (count_one_in, count_one),
        (bias_one_in, bias_one),
        (self_two_in, self_two),
        (neigh_two_in, neigh_two),
        (bias_two_in, bias_two),
        (cotangent_in, cotangent),
        (nbr_two_in, nbr_two),
        (count_two_in, count_two),
        (nbr_one_in, nbr_one),
    )
    loads += [
        pltpu.make_async_copy(src, dst, load_sem.at[4 + i]) for i, (src, dst) in enumerate(pairs)
    ]
    for load in loads:
        load.start()

    loads[4].wait()
    loads[5].wait()
    cols_mine = pl.ds(pl.multiple_of(core * 256, 256), 256)
    weights_one[z, rows(chip, 16), cols_mine] = weights_mine[rows(chip, 16), cols_mine]
    pl.semaphore_wait(barrier, len(everyone))

    part = weights_one.at[z, rows(chip, 16), cols_mine]
    pending_weights = [send(weights_mine.at[rows(chip, 16), cols_mine], part, at_z(p)) for p in z_peers]
    pending_own = []
    for p in z_peers:
        pending_own.append(
            send(features_in.at[rows(p, OWN_SEEDS), :], own_in.at[pl.ds(0, OWN_SEEDS), lanes(2 * z)], at_z(p))
        )
        pending_own.append(
            send(
                features_in.at[rows(p, REST, SEEDS), :],
                own_in.at[pl.ds(OWN_SEEDS, REST), lanes(2 * z)],
                at_z(p),
            )
        )

    def widen(i, carry):
        block = pl.ds(pl.multiple_of(i * 256, 256), 256)
        table[block, :] = features[block, :].astype(F32)
        return carry

    table[pl.ds(SOURCES, 8), :] = jnp.zeros((8, COLS), F32)
    steps = quarter // 256
    for i in range(4):
        loads[i].wait()
        lax.fori_loop(i * steps, (i + 1) * steps, widen, 0)
    own_in[pl.ds(0, OWN_SEEDS), lanes(2 * z)] = features[rows(z, OWN_SEEDS), :]
    own_in[pl.ds(OWN_SEEDS, REST), lanes(2 * z)] = features[rows(z, REST, SEEDS), :]
    for load in loads[6:]:
        load.wait()

    lists = []
    for k in range(FAN_ONE):
        masked[k] = jnp.where(count_one[...] > k, nbr_one[k : k + 1, :], SOURCES)
        lists.append(pltpu.make_async_copy(masked.at[k, 0], index_one[k], load_sem.at[15 + k]))
        lists[-1].start()

    for i in range(MIDDLE // 128):
        line = 1.0 / count_one[:, i * 128 : (i + 1) * 128].astype(F32)
        inverse_one[i * 128 : (i + 1) * 128, :] = jnp.broadcast_to(line, (128, 128)).T
    for copy in lists:
        copy.wait()

    wait(pending_weights)
    part = weights_one.at[:, rows(chip, 16), cols_mine]
    pending_weights = [send(part, part, at_plane(p)) for p in plane_peers]

    for turn, d in enumerate((4, 3, 5, 2, 6, 1, 7, 0)):
        owner = (z + d) % Z

        def gather(g, carry, owner=owner):
            seed_base = owner * OWN_SEEDS + g * GROUP
            rest_base = SEEDS - OWN_SEEDS + owner * REST + g * GROUP
            base = jnp.where(g < OWN_SEEDS // GROUP, seed_base, rest_base)
            out = pl.multiple_of(g * GROUP, GROUP)
            for j in range(GROUP):
                terms = [table[pl.ds(index_one[k][base + j], 1), :] for k in range(FAN_ONE)]
                total_one[pl.ds(out + j, 1), :] = tree_sum(terms)
            return carry

        lax.fori_loop(0, OWN // GROUP, gather, 0)
        seeds = total_one[pl.ds(0, OWN_SEEDS), :] * inverse_one[rows(owner, OWN_SEEDS), :]
        rest = total_one[pl.ds(OWN_SEEDS, REST), :] * inverse_one[rows(owner, REST, SEEDS), :]
        if d:
            mean_one[turn, pl.ds(0, OWN_SEEDS), :] = seeds.astype(BF16)
            mean_one[turn, pl.ds(OWN_SEEDS, REST), :] = rest.astype(BF16)
            pending_own.append(send(mean_one.at[turn], own_in.at[:, lanes(2 * z + 1)], at_z(owner)))
        else:
            own_in[pl.ds(0, OWN_SEEDS), lanes(2 * z + 1)] = seeds.astype(BF16)
            own_in[pl.ds(OWN_SEEDS, REST), lanes(2 * z + 1)] = rest.astype(BF16)
        if turn == 5:
            wait(pending_weights)
            part = weights_one.at[:, :, cols_mine]
            pending_weights = [send(part, part, sibling)]
    wait(pending_weights)
    wait(pending_own)

    def layer_one(d, carry):
        cols = lanes((col + d) % 4)
        pre = dot(own_in[...], weights_one[:, :, cols].reshape(2 * Z * COLS, 128)) + bias_one[:, cols]
        act_own[:, cols] = jax.nn.softplus(pre).astype(BF16)
        return carry

    pending = []
    for d in (2, 1, 3):
        lax.fori_loop(d, d + 1, layer_one, 0)
        p = (col + d) % 4
        pending.append(send(act_own.at[:, lanes(p)], act_cols.at[rows(col, OWN), :], at_z(half * 4 + p)))
    lax.fori_loop(0, 1, layer_one, 0)
    act_cols[rows(col, OWN), :] = act_own[:, lanes(col)]

    index_two = [
        jnp.where(count_two[...] > k, nbr_two[k : k + 1, :], -1) for k in range(FAN_TWO)
    ]
    inverse = 1.0 / count_two[...].astype(F32)
    inverse_two[...] = jnp.broadcast_to(inverse, (128, SEEDS)).T

    def count_block(i, carry):
        spot = lax.broadcasted_iota(jnp.int32, (64, SEEDS), 0) + (i % 4) * 64
        block = half * 4 + i // 4
        node = jnp.where(spot < OWN_SEEDS, block * OWN_SEEDS + spot, SEEDS - OWN_SEEDS + block * REST + spot)
        total = jnp.zeros((64, SEEDS), F32)
        for k in range(FAN_TWO):
            total = total + jnp.where(node == index_two[k], 1.0, 0.0)
        counts[rows(i, 64), :] = total.astype(BF16)
        return carry

    lax.fori_loop(0, 16, count_block, 0)
    wait(pending)

    share = dot_tn(act_cols[...], counts[...])
    mean_send[...] = (share.T * inverse_two[...]).astype(BF16)
    pending = [send(mean_send.at[rows(p, OWN_SEEDS), :], mean_land.at[z], at_z(p)) for p in z_peers]
    mean_land[z] = mean_send[rows(z, OWN_SEEDS), :]
    pre_self = dot(act_own[pl.ds(0, OWN_SEEDS), :], self_two[...]) + bias_two[...]

    def turn_block(t, carry):
        own_in_t[rows(t, 128), :] = own_in[:, lanes(t)].T
        return carry

    lax.fori_loop(0, 2 * Z, turn_block, 0)
    wait(pending)
    for q in range(4):
        both = mean_land[q].astype(F32) + mean_land[4 + q].astype(F32)
        mean_two[:, q * 128 : (q + 1) * 128] = both.astype(BF16)

    pre_two = pre_self + dot(mean_two[...], neigh_two[...])
    slope = cotangent[...].astype(F32) * jax.nn.sigmoid(pre_two)
    slope_two[...] = slope.astype(BF16)

    spread = dot_nt(slope_two[...], neigh_two[...])
    inverse = inverse_two[rows(z, OWN_SEEDS), :]
    for q in range(4):
        cols = slice(q * 128, (q + 1) * 128)
        spread_send[:, cols] = (spread[:, cols] * inverse).astype(BF16)
    pending = [
        send(spread_send.at[:, lanes(p % 4)], spread_cols.at[rows(z, OWN_SEEDS), :], at_z(p)) for p in z_peers
    ]
    spread_cols[rows(z, OWN_SEEDS), :] = spread_send[:, lanes(col)]

    own_two = act_own[pl.ds(0, OWN_SEEDS), :]
    keep_self = jnp.where(core == 0, 1.0, 0.0).astype(BF16)
    keep_neigh = jnp.where(core == 0, 0.0, 1.0).astype(BF16)
    mixed_send = own_two * keep_neigh + mean_two[...] * keep_self
    mixed_keep = own_two * keep_self + mean_two[...] * keep_neigh
    g2_send[...] = dot_tn(mixed_send, slope_two[...]).astype(BF16)
    pending_g2 = [send(g2_send, g2_core, sibling)]
    g2_keep[...] = dot_tn(mixed_keep, slope_two[...])

    def direct_block(n, carry):
        cols = pl.ds(pl.multiple_of(n * 256, 256), 256)
        direct[:, cols] = dot_nt(slope_two[...], self_two[cols, :])
        return carry

    lax.fori_loop(0, 2, direct_block, 0)
    bias_two_sum = jnp.sum(slope_two[...].astype(F32), axis=0, keepdims=True)
    wait(pending)

    def scatter_block(d, carry):
        block = rows((col + d) % 4, OWN)
        scat_send[block, :] = dot(counts[block, :], spread_cols[...]).astype(BF16)
        return carry

    pending = []
    for first in (2, 0):
        lax.fori_loop(first, first + 2, scatter_block, 0)
        for d in (2, 3) if first else (1,):
            p = (col + d) % 4
            part = scat_send.at[rows(p, OWN), :]
            pending.append(send(part, scat_own.at[:, lanes(col)], at_z(half * 4 + p)))
    scat_own[:, lanes(col)] = scat_send[rows(col, OWN), :]
    wait(pending_g2)

    def g2_pair(i, carry):
        block = rows(i, 128)
        g2_sum[block, :] = (g2_keep[block, :] + g2_core[block, :].astype(F32)).astype(BF16)
        return carry

    lax.fori_loop(0, 4, g2_pair, 0)
    pending_g2 = [
        send(g2_sum.at[rows(p[1], 128), lanes(p[0])], g2_plane.at[chip], at_plane(p)) for p in plane_peers
    ]
    g2_plane[chip] = g2_sum[rows(y, 128), lanes(x)]
    wait(pending)

    back = scat_own[pl.ds(0, OWN_SEEDS), :].astype(F32) + direct[...]
    gate = 1.0 - jnp.exp(-act_own[pl.ds(0, OWN_SEEDS), :].astype(F32))
    slope_one[pl.ds(0, OWN_SEEDS), :] = (back * gate).astype(BF16)
    back = scat_own[pl.ds(OWN_SEEDS, REST), :].astype(F32)
    gate = 1.0 - jnp.exp(-act_own[pl.ds(OWN_SEEDS, REST), :].astype(F32))
    slope_one[pl.ds(OWN_SEEDS, REST), :] = (back * gate).astype(BF16)

    def g1_block(t, carry):
        g1_send[t] = dot(own_in_t[rows(2 * t + other, 128), :], slope_one[...]).astype(BF16)
        return carry

    pending = []
    for part in range(2):
        lax.fori_loop(part * 4, part * 4 + 4, g1_block, 0)
        chunk = pl.ds(part * 4, 4)
        pending.append(send(g1_send.at[chunk], g1_core.at[chunk], sibling))

    def g1_own(t, carry):
        g1_keep[t] = dot(own_in_t[rows(2 * t + core, 128), :], slope_one[...])
        return carry

    def g1_pair(t, carry):
        both = g1_keep[t] + g1_core[t].astype(F32)
        g1_sum[t] = both.astype(BF16).reshape(4, 32, HID)
        return carry

    lax.fori_loop(0, 4, g1_own, 0)
    wait(pending[:1])
    lax.fori_loop(0, 4, g1_pair, 0)
    low, high = pl.ds(0, 4), pl.ds(4, 4)
    pending_x = [
        send(g1_sum.at[low, :, :, lanes(p)], g1_first_x.at[x], at_plane((p, y))) for p in ring_peers(x)
    ]
    g1_first_x[x] = g1_sum[0:4, :, :, lanes(x)]
    lax.fori_loop(4, 8, g1_own, 0)
    wait(pending[1:])
    lax.fori_loop(4, 8, g1_pair, 0)
    pending_y = [send(g1_sum.at[high, p], g1_first_y.at[y], at_plane((x, p))) for p in ring_peers(y)]
    g1_first_y[y] = g1_sum[4:8, y]

    bias_one_sum = jnp.sum(slope_one[...].astype(F32), axis=0, keepdims=True)
    for i in range(4):
        bias_mine[i : i + 1, :] = bias_one_sum[:, i * 128 : (i + 1) * 128]
        bias_mine[4 + i : 5 + i, :] = bias_two_sum[:, i * 128 : (i + 1) * 128]
    pending_bias = [send(bias_mine, bias_core, sibling)]

    wait(pending_g2)
    total = tree_sum([g2_plane[p].astype(F32) for p in range(16)])
    g2_piece[...] = total.astype(BF16)
    pending_g2 = [send(g2_piece.at[rows(p, 16), :], g2_z.at[z], at_z(p)) for p in z_peers]
    g2_z[z] = g2_piece[rows(z, 16), :]
    wait(pending_g2)
    total = tree_sum([g2_z[p].astype(F32) for p in range(Z)])
    g2_row[rows(z, 16), :] = total.astype(BF16)
    pending_g2 = [send(g2_row.at[rows(z, 16), :], g2_row.at[rows(z, 16), :], at_z(p)) for p in z_peers]
    wait(pending_bias)
    bias_pair[...] = bias_mine[...] + bias_core[...]
    pending_bias = [send(bias_pair, bias_x.at[x], at_plane((p, y))) for p in ring_peers(x)]
    bias_x[x] = bias_pair[...]

    wait(pending_x)

    def g1_over_x(t, carry):
        total = tree_sum([g1_first_x[p, t].astype(F32) for p in range(4)])
        g1_part_x[t] = total.astype(BF16)
        return carry

    lax.fori_loop(0, 4, g1_over_x, 0)
    pending_x = [send(g1_part_x.at[:, p], g1_then_y.at[y], at_plane((x, p))) for p in ring_peers(y)]
    g1_then_y[y] = g1_part_x[:, y]
    wait(pending_y)

    def g1_over_y(t, carry):
        total = tree_sum([g1_first_y[p, t].astype(F32) for p in range(4)])
        g1_part_y[t] = total.astype(BF16)
        return carry

    lax.fori_loop(0, 4, g1_over_y, 0)
    pending_y = [
        send(g1_part_y.at[:, :, lanes(p)], g1_then_x.at[x], at_plane((p, y))) for p in ring_peers(x)
    ]
    g1_then_x[x] = g1_part_y[:, :, lanes(x)]
    wait(pending_bias)
    bias_row[...] = tree_sum([bias_x[p] for p in range(4)])
    pending_bias = [send(bias_row, bias_y.at[y], at_plane((x, p))) for p in ring_peers(y)]
    bias_y[y] = bias_row[...]
    wait(pending_g2)
    pending_g2 = [
        send(g2_row, out_two.at[core, rows(y, 128), lanes(x)], at_plane(p)) for p in plane_peers
    ]
    out_two[core, rows(y, 128), lanes(x)] = g2_row[...]
    wait(pending_x)
    wait(pending_y)

    def g1_chips(t, carry):
        g1_piece[t] = tree_sum([g1_then_y[p, t].astype(F32) for p in range(4)]).astype(BF16)
        g1_piece[4 + t] = tree_sum([g1_then_x[p, t].astype(F32) for p in range(4)]).astype(BF16)
        return carry

    lax.fori_loop(0, 4, g1_chips, 0)
    pending = [send(g1_piece.at[p], g1_z.at[z], at_z(p)) for p in z_peers]
    g1_z[z] = g1_piece[z]
    wait(pending_bias)
    bias_chips[...] = tree_sum([bias_y[p] for p in range(4)])
    pending_bias = [send(bias_chips, bias_z.at[z], at_z(p)) for p in z_peers]
    bias_z[z] = bias_chips[...]
    wait(pending)
    total = tree_sum([g1_z[p].astype(F32) for p in range(Z)])
    out_one[core, rows(y, 32), lanes(x)] = total.astype(BF16)

    mine = out_one.at[core, rows(y, 32), lanes(x)]
    pending = [send(mine, mine, at_plane(p)) for p in plane_peers]
    wait(pending_g2)
    pending_g2 = [send(out_two.at[core], out_two.at[core], sibling)]
    wait(pending_bias)
    total = tree_sum([bias_z[p] for p in range(Z)])
    for i in range(4):
        result_bias_one[:, i * 128 : (i + 1) * 128] = total[i : i + 1, :]
        result_bias_two[:, i * 128 : (i + 1) * 128] = total[4 + i : 5 + i, :]
    wait(pending)
    pending = [send(out_one.at[core], out_one.at[core], sibling)]
    wait(pending_g2)
    stores = [
        pltpu.make_async_copy(out_two.at[0], result_self_two, load_sem.at[0]),
        pltpu.make_async_copy(out_two.at[1], result_neigh_two, load_sem.at[1]),
        pltpu.make_async_copy(out_one.at[0], result_self_one, load_sem.at[2]),
        pltpu.make_async_copy(out_one.at[1], result_neigh_one, load_sem.at[3]),
    ]
    stores[0].start()
    stores[1].start()
    wait(pending)
    stores[2].start()
    stores[3].start()
    for store in stores:
        store.wait()
    assert len(used) <= N_COPIES


def training_step(*operands):
    bf16 = [
        jnp.int32,
        jnp.int32,
        (2, 128, HID),
        (2, HID, HID),
        (2 * Z * COLS, OWN),
        (SOURCES, COLS),
        jnp.int32,
        None,
        (HID, HID),
        (HID, HID),
        None,
        (OWN_SEEDS, HID),
        jnp.int32,
        jnp.int32,
        None,
        None,
        None,
        None,
        (Z - 1, OWN, COLS),
        (2 * COLS, HID),
        (Z, 2 * COLS, HID),
        (OWN, 2 * Z * COLS),
        (OWN, HID),
        (4 * OWN, 128),
        (4 * OWN, SEEDS),
        (SEEDS, 128),
        (Z, OWN_SEEDS, 128),
        (OWN_SEEDS, HID),
        (OWN_SEEDS, HID),
        (OWN_SEEDS, HID),
        (SEEDS, 128),
        None,
        (4 * OWN, 128),
        (OWN, HID),
        (OWN, HID),
        None,
        (HID, HID),
        (HID, HID),
        (HID, HID),
        (16, 128, 128),
        (128, 128),
        (Z, 16, 128),
        (128, 128),
        None,
        (Z, 128, HID),
        (Z, 128, HID),
        (Z, 4, 32, HID),
        (4, 4, 4, 32, 128),
        (4, 4, 32, 128),
        (4, 4, 32, 128),
        (4, 4, 32, HID),
        (4, 32, HID),
        (4, 4, 32, 128),
        (Z, 32, 128),
        (Z, 32, 128),
    ]
    wide = iter(
        [
            (1, HID),
            (1, HID),
            (MIDDLE, 128),
            (SEEDS, 128),
            (SOURCES + 8, COLS),
            (OWN, COLS),
            (OWN_SEEDS, HID),
            (HID, HID),
            (Z, 128, HID),
        ]
    )
    whole = iter([(FAN_ONE, 1, MIDDLE), (FAN_ONE, MIDDLE), (1, MIDDLE), (FAN_TWO, SEEDS), (1, SEEDS)])
    scratch = [[pltpu.SMEM((MIDDLE,), jnp.int32) for k in range(FAN_ONE)]]
    for entry in bf16:
        if entry is None:
            scratch.append(pltpu.VMEM(next(wide), F32))
        elif entry is jnp.int32:
            scratch.append(pltpu.VMEM(next(whole), jnp.int32))
        else:
            scratch.append(pltpu.VMEM(entry, BF16))
    tile = (8, 128)
    four = (4, *tile)
    scratch += [pltpu.VMEM(s, F32) for s in (tile, tile, tile, four, tile, four, tile, (Z, *tile))]
    scratch += [pltpu.SemaphoreType.DMA((N_COPIES,)), pltpu.SemaphoreType.DMA((N_COPIES,))]
    scratch += [pltpu.SemaphoreType.DMA((15 + FAN_ONE,))]
    return pl.pallas_call(
        step_kernel,
        name="training_step",
        out_shape=(
            jax.ShapeDtypeStruct((128, HID), BF16),
            jax.ShapeDtypeStruct((128, HID), BF16),
            jax.ShapeDtypeStruct((HID, HID), BF16),
            jax.ShapeDtypeStruct((HID, HID), BF16),
            jax.ShapeDtypeStruct((1, HID), F32),
            jax.ShapeDtypeStruct((1, HID), F32),
        ),
        in_specs=[HBM] * len(operands),
        out_specs=(HBM, HBM, HBM, HBM, VMEM, VMEM),
        scratch_shapes=scratch,
        compiler_params=pltpu.CompilerParams(
            collective_id=0, has_side_effects=True, vmem_limit_bytes=60 << 20
        ),
    )(*operands)


def widen_kernel(*refs):
    half = len(refs) // 2
    for narrow, wide in zip(refs[:half], refs[half:]):
        wide[...] = narrow[...].astype(F32)


def widen_all(*arrays):
    steps = 2
    specs = [
        pl.BlockSpec((a.shape[0] // steps, HID), lambda i: (i, 0))
        if a.shape[0] > 1
        else pl.BlockSpec((1, HID), lambda i: (0, 0))
        for a in arrays
    ]
    return pl.pallas_call(
        widen_kernel,
        name="widen",
        grid=(steps,),
        out_shape=[jax.ShapeDtypeStruct(a.shape, F32) for a in arrays],
        in_specs=specs,
        out_specs=specs,
        compiler_params=pltpu.CompilerParams(vmem_limit_bytes=60 << 20),
    )(*arrays)


def on_device(
    features,
    nbr_one,
    count_one,
    nbr_two,
    count_two,
    self_one,
    neigh_one,
    bias_one,
    self_two,
    neigh_two,
    bias_two,
    cotangent,
):
    sums = training_step(
        nbr_one,
        features,
        count_one[None, :],
        self_one,
        neigh_one,
        bias_one[None, :],
        self_two,
        neigh_two,
        bias_two[None, :],
        cotangent,
        nbr_two,
        count_two[None, :],
    )
    g_self_one, g_neigh_one, g_self_two, g_neigh_two, g_bias_one, g_bias_two = widen_all(*sums)
    return (
        g_self_one,
        g_neigh_one,
        g_bias_one.reshape(HID),
        g_self_two,
        g_neigh_two,
        g_bias_two.reshape(HID),
    )


def solution(mesh):
    in_specs = (
        P("batch", "feat"),
        P(None, "batch"),
        P("batch"),
        P(None, "batch"),
        P("batch"),
        P("feat", None),
        P("feat", None),
        P(),
        P(),
        P(),
        P(),
        P(("batch", "feat"), None),
    )
    out_specs = (P("feat", None), P("feat", None), P(), P(), P(), P())
    return jax.shard_map(
        on_device, mesh=mesh, in_specs=in_specs, out_specs=out_specs, check_vma=False
    )
```

```python
import functools

import jax
import jax.numpy as jnp
from jax import lax
from jax.experimental import pallas as pl
from jax.experimental.pallas import tpu as pltpu
from jax.sharding import PartitionSpec as P

MESH = pl.DeviceIdType.MESH
F32 = jnp.float32
BF16 = jnp.bfloat16
VMEM = pl.BlockSpec(memory_space=pltpu.VMEM)
HBM = pl.BlockSpec(memory_space=pltpu.HBM)

SOURCES = 8192
MIDDLE = 2048
SEEDS = 512
HID = 512
COLS = 128
FAN_ONE = 15
FAN_TWO = 10
Z = 8
OWN = 256
OWN_SEEDS = 64
REST = 192
GROUP = 32


def tree_sum(terms):
    while len(terms) > 1:
        odd = [terms[-1]] if len(terms) % 2 else []
        terms = [a + b for a, b in zip(terms[::2], terms[1::2])] + odd
    return terms[0]


def dot(a, b):
    return jnp.dot(a, b, preferred_element_type=F32)


def dot_tn(a, b):
    return lax.dot_general(a, b, (((0,), (0,)), ((), ())), preferred_element_type=F32)


def dot_nt(a, b):
    return lax.dot_general(a, b, (((1,), (1,)), ((), ())), preferred_element_type=F32)


N_COPIES = 200


def step_kernel(
    nbr_one_in,
    features_in,
    count_one_in,
    self_one,
    neigh_one,
    bias_one_in,
    self_two_in,
    neigh_two_in,
    bias_two_in,
    cotangent_in,
    nbr_two_in,
    count_two_in,
    result_self_one,
    result_neigh_one,
    result_self_two,
    result_neigh_two,
    result_bias_one,
    result_bias_two,
    index_one,
    masked,
    nbr_one,
    out_one,
    out_two,
    own_in_t,
    features,
    count_one,
    bias_one,
    self_two,
    neigh_two,
    bias_two,
    cotangent,
    nbr_two,
    count_two,
    inverse_one,
    inverse_two,
    table,
    total_one,
    mean_one,
    weights_mine,
    weights_one,
    own_in,
    act_own,
    act_cols,
    counts,
    mean_send,
    mean_land,
    mean_two,
    slope_two,
    spread_send,
    spread_cols,
    direct,
    scat_send,
    scat_own,
    slope_one,
    g2_keep,
    g2_send,
    g2_core,
    g2_sum,
    g2_plane,
    g2_piece,
    g2_z,
    g2_row,
    g1_keep,
    g1_send,
    g1_core,
    g1_sum,
    g1_first_x,
    g1_part_x,
    g1_then_y,
    g1_first_y,
    g1_part_y,
    g1_then_x,
    g1_piece,
    g1_z,
    bias_mine,
    bias_core,
    bias_pair,
    bias_x,
    bias_row,
    bias_y,
    bias_chips,
    bias_z,
    send_sem,
    recv_sem,
    load_sem,
):
    b = lax.axis_index("batch")
    z = lax.axis_index("feat")
    core = b % 2
    x = (b // 2) % 4
    y = b // 8
    half = z // 4
    col = z % 4
    chip = y * 4 + x
    other = 1 - core
    sibling = {"batch": b + 1 - 2 * core, "feat": z}
    z_peers = [(z + d) % Z for d in (4, 3, 5, 2, 6, 1, 7)]
    ring_peers = lambda place: [(place + d) % 4 for d in range(1, 4)]
    half_peers = [(col + d) % 4 for d in range(1, 4)]
    plane_peers = [((x + d % 4) % 4, (y + d // 4) % 4) for d in range(1, 16)]

    def at_z(peer):
        return {"batch": b, "feat": peer}

    def at_plane(peer):
        return {"batch": peer[1] * 8 + peer[0] * 2 + core, "feat": z}

    used = []

    def send(src, dst, device):
        number = len(used)
        used.append(number)
        copy = pltpu.make_async_remote_copy(
            src_ref=src,
            dst_ref=dst,
            send_sem=send_sem.at[number],
            recv_sem=recv_sem.at[number],
            device_id=device,
            device_id_type=MESH,
        )
        copy.start()
        return copy

    def wait(copies):
        for copy in copies:
            copy.wait()

    def lanes(number, start=0):
        return pl.ds(pl.multiple_of(start + number * 128, 128), 128)

    def rows(number, size, start=0):
        return pl.ds(pl.multiple_of(start + number * size, 16), size)

    barrier = pltpu.get_barrier_semaphore()
    everyone = [at_z(p) for p in z_peers] + [at_plane(p) for p in plane_peers] + [sibling]
    for device in everyone:
        pl.semaphore_signal(barrier, inc=1, device_id=device, device_id_type=MESH)
    quarter = SOURCES // 4
    loads = [
        pltpu.make_async_copy(
            features_in.at[pl.ds(i * quarter, quarter), :],
            features.at[pl.ds(i * quarter, quarter), :],
            load_sem.at[i],
        )
        for i in range(4)
    ]
    pairs = (
        (self_one, weights_mine.at[pl.ds(0, COLS), :]),
        (neigh_one, weights_mine.at[pl.ds(COLS, COLS), :]),
        (count_one_in, count_one),
        (bias_one_in, bias_one),
        (self_two_in, self_two),
        (neigh_two_in, neigh_two),
        (bias_two_in, bias_two),
        (cotangent_in, cotangent),
        (nbr_two_in, nbr_two),
        (count_two_in, count_two),
        (nbr_one_in, nbr_one),
    )
    loads += [
        pltpu.make_async_copy(src, dst, load_sem.at[4 + i]) for i, (src, dst) in enumerate(pairs)
    ]
    for load in loads:
        load.start()

    loads[4].wait()
    loads[5].wait()
    cols_mine = pl.ds(pl.multiple_of(core * 256, 256), 256)
    weights_one[z, rows(chip, 16), cols_mine] = weights_mine[rows(chip, 16), cols_mine]
    pl.semaphore_wait(barrier, len(everyone))

    part = weights_one.at[z, rows(chip, 16), cols_mine]
    pending_weights = [send(weights_mine.at[rows(chip, 16), cols_mine], part, at_z(p)) for p in z_peers]
    pending_own = []
    for p in z_peers:
        pending_own.append(
            send(features_in.at[rows(p, OWN_SEEDS), :], own_in.at[pl.ds(0, OWN_SEEDS), lanes(2 * z)], at_z(p))
        )
        pending_own.append(
            send(
                features_in.at[rows(p, REST, SEEDS), :],
                own_in.at[pl.ds(OWN_SEEDS, REST), lanes(2 * z)],
                at_z(p),
            )
        )

    loads[6].wait()
    loads[14].wait()

    lists = []
    for k in range(FAN_ONE):
        masked[k] = jnp.where(count_one[...] > k, nbr_one[k : k + 1, :], SOURCES)
        lists.append(pltpu.make_async_copy(masked.at[k, 0], index_one[k], load_sem.at[15 + k]))
        lists[-1].start()

    def widen(i, carry):
        block = pl.ds(pl.multiple_of(i * 256, 256), 256)
        table[block, :] = features[block, :].astype(F32)
        return carry

    table[pl.ds(SOURCES, 8), :] = jnp.zeros((8, COLS), F32)
    steps = quarter // 256
    for i in range(4):
        loads[i].wait()
        lax.fori_loop(i * steps, (i + 1) * steps, widen, 0)
    own_in[pl.ds(0, OWN_SEEDS), lanes(2 * z)] = features[rows(z, OWN_SEEDS), :]
    own_in[pl.ds(OWN_SEEDS, REST), lanes(2 * z)] = features[rows(z, REST, SEEDS), :]
    for i in range(MIDDLE // 128):
        line = 1.0 / count_one[:, i * 128 : (i + 1) * 128].astype(F32)
        inverse_one[i * 128 : (i + 1) * 128, :] = jnp.broadcast_to(line, (128, 128)).T
    for copy in lists:
        copy.wait()

    wait(pending_weights)
    part = weights_one.at[:, rows(chip, 16), cols_mine]
    pending_weights = [send(part, part, at_plane(p)) for p in plane_peers]

    for turn, d in enumerate((4, 3, 5, 2, 6, 1, 7, 0)):
        owner = (z + d) % Z

        def gather(g, carry, owner=owner):
            seed_base = owner * OWN_SEEDS + g * GROUP
            rest_base = SEEDS - OWN_SEEDS + owner * REST + g * GROUP
            base = jnp.where(g < OWN_SEEDS // GROUP, seed_base, rest_base)
            out = pl.multiple_of(g * GROUP, GROUP)
            for j in range(GROUP):
                terms = [table[pl.ds(index_one[k][base + j], 1), :] for k in range(FAN_ONE)]
                total_one[pl.ds(out + j, 1), :] = tree_sum(terms)
            return carry

        lax.fori_loop(0, OWN // GROUP, gather, 0)
        seeds = total_one[pl.ds(0, OWN_SEEDS), :] * inverse_one[rows(owner, OWN_SEEDS), :]
        rest = total_one[pl.ds(OWN_SEEDS, REST), :] * inverse_one[rows(owner, REST, SEEDS), :]
        if d:
            mean_one[turn, pl.ds(0, OWN_SEEDS), :] = seeds.astype(BF16)
            mean_one[turn, pl.ds(OWN_SEEDS, REST), :] = rest.astype(BF16)
            pending_own.append(send(mean_one.at[turn], own_in.at[:, lanes(2 * z + 1)], at_z(owner)))
        else:
            own_in[pl.ds(0, OWN_SEEDS), lanes(2 * z + 1)] = seeds.astype(BF16)
            own_in[pl.ds(OWN_SEEDS, REST), lanes(2 * z + 1)] = rest.astype(BF16)
        if turn == 5:
            wait(pending_weights)
            part = weights_one.at[:, :, cols_mine]
            pending_weights = [send(part, part, sibling)]
    for i in range(7, 14):
        loads[i].wait()
    wait(pending_weights)
    wait(pending_own)

    def layer_one(d, carry):
        cols = lanes((col + d) % 4)
        pre = dot(own_in[...], weights_one[:, :, cols].reshape(2 * Z * COLS, 128)) + bias_one[:, cols]
        act_own[:, cols] = jax.nn.softplus(pre).astype(BF16)
        return carry

    pending = []
    for d in (2, 1, 3):
        lax.fori_loop(d, d + 1, layer_one, 0)
        p = (col + d) % 4
        pending.append(send(act_own.at[:, lanes(p)], act_cols.at[rows(col, OWN), :], at_z(half * 4 + p)))
    lax.fori_loop(0, 1, layer_one, 0)
    act_cols[rows(col, OWN), :] = act_own[:, lanes(col)]

    index_two = [
        jnp.where(count_two[...] > k, nbr_two[k : k + 1, :], -1) for k in range(FAN_TWO)
    ]
    inverse = 1.0 / count_two[...].astype(F32)
    inverse_two[...] = jnp.broadcast_to(inverse, (128, SEEDS)).T

    def count_block(i, carry):
        spot = lax.broadcasted_iota(jnp.int32, (64, SEEDS), 0) + (i % 4) * 64
        block = half * 4 + i // 4
        node = jnp.where(spot < OWN_SEEDS, block * OWN_SEEDS + spot, SEEDS - OWN_SEEDS + block * REST + spot)
        total = jnp.zeros((64, SEEDS), F32)
        for k in range(FAN_TWO):
            total = total + jnp.where(node == index_two[k], 1.0, 0.0)
        counts[rows(i, 64), :] = total.astype(BF16)
        return carry

    lax.fori_loop(0, 16, count_block, 0)
    wait(pending)

    share = dot_tn(act_cols[...], counts[...])
    mean_send[...] = (share.T * inverse_two[...]).astype(BF16)
    pending = [send(mean_send.at[rows(p, OWN_SEEDS), :], mean_land.at[z], at_z(p)) for p in z_peers]
    mean_land[z] = mean_send[rows(z, OWN_SEEDS), :]
    pre_self = dot(act_own[pl.ds(0, OWN_SEEDS), :], self_two[...]) + bias_two[...]

    def turn_block(t, carry):
        own_in_t[rows(t, 128), :] = own_in[:, lanes(t)].T
        return carry

    lax.fori_loop(0, 2 * Z, turn_block, 0)
    wait(pending)
    for q in range(4):
        both = mean_land[q].astype(F32) + mean_land[4 + q].astype(F32)
        mean_two[:, q * 128 : (q + 1) * 128] = both.astype(BF16)

    pre_two = pre_self + dot(mean_two[...], neigh_two[...])
    slope = cotangent[...].astype(F32) * jax.nn.sigmoid(pre_two)
    slope_two[...] = slope.astype(BF16)

    spread = dot_nt(slope_two[...], neigh_two[...])
    inverse = inverse_two[rows(z, OWN_SEEDS), :]
    for q in range(4):
        cols = slice(q * 128, (q + 1) * 128)
        spread_send[:, cols] = (spread[:, cols] * inverse).astype(BF16)
    pending = [
        send(spread_send.at[:, lanes(p % 4)], spread_cols.at[rows(z, OWN_SEEDS), :], at_z(p)) for p in z_peers
    ]
    spread_cols[rows(z, OWN_SEEDS), :] = spread_send[:, lanes(col)]

    own_two = act_own[pl.ds(0, OWN_SEEDS), :]
    keep_self = jnp.where(core == 0, 1.0, 0.0).astype(BF16)
    keep_neigh = jnp.where(core == 0, 0.0, 1.0).astype(BF16)
    mixed_send = own_two * keep_neigh + mean_two[...] * keep_self
    mixed_keep = own_two * keep_self + mean_two[...] * keep_neigh
    g2_send[...] = dot_tn(mixed_send, slope_two[...]).astype(BF16)
    pending_g2 = [send(g2_send, g2_core, sibling)]
    g2_keep[...] = dot_tn(mixed_keep, slope_two[...])

    def direct_block(n, carry):
        cols = pl.ds(pl.multiple_of(n * 256, 256), 256)
        direct[:, cols] = dot_nt(slope_two[...], self_two[cols, :])
        return carry

    lax.fori_loop(0, 2, direct_block, 0)
    bias_two_sum = jnp.sum(slope_two[...].astype(F32), axis=0, keepdims=True)
    wait(pending_g2)

    def g2_pair(i, carry):
        block = rows(i, 128)
        g2_sum[block, :] = (g2_keep[block, :] + g2_core[block, :].astype(F32)).astype(BF16)
        return carry

    lax.fori_loop(0, 4, g2_pair, 0)
    pending_g2 = [
        send(g2_sum.at[rows(p[1], 128), lanes(p[0])], g2_plane.at[chip], at_plane(p)) for p in plane_peers
    ]
    g2_plane[chip] = g2_sum[rows(y, 128), lanes(x)]
    wait(pending)

    def scatter_block(d, carry):
        block = rows((col + d) % 4, OWN)
        scat_send[block, :] = dot(counts[block, :], spread_cols[...]).astype(BF16)
        return carry

    pending = []
    for first in (2, 0):
        lax.fori_loop(first, first + 2, scatter_block, 0)
        for d in (2, 3) if first else (1,):
            p = (col + d) % 4
            part = scat_send.at[rows(p, OWN), :]
            pending.append(send(part, scat_own.at[:, lanes(col)], at_z(half * 4 + p)))
    scat_own[:, lanes(col)] = scat_send[rows(col, OWN), :]
    wait(pending)

    back = scat_own[pl.ds(0, OWN_SEEDS), :].astype(F32) + direct[...]
    gate = 1.0 - jnp.exp(-act_own[pl.ds(0, OWN_SEEDS), :].astype(F32))
    slope_one[pl.ds(0, OWN_SEEDS), :] = (back * gate).astype(BF16)
    back = scat_own[pl.ds(OWN_SEEDS, REST), :].astype(F32)
    gate = 1.0 - jnp.exp(-act_own[pl.ds(OWN_SEEDS, REST), :].astype(F32))
    slope_one[pl.ds(OWN_SEEDS, REST), :] = (back * gate).astype(BF16)

    def g1_block(t, carry):
        g1_send[t] = dot(own_in_t[rows(2 * t + other, 128), :], slope_one[...]).astype(BF16)
        return carry

    pending = []
    for part in range(2):
        lax.fori_loop(part * 4, part * 4 + 4, g1_block, 0)
        chunk = pl.ds(part * 4, 4)
        pending.append(send(g1_send.at[chunk], g1_core.at[chunk], sibling))

    def g1_own(t, carry):
        g1_keep[t] = dot(own_in_t[rows(2 * t + core, 128), :], slope_one[...])
        return carry

    def g1_pair(t, carry):
        both = g1_keep[t] + g1_core[t].astype(F32)
        g1_sum[t] = both.astype(BF16).reshape(4, 32, HID)
        return carry

    lax.fori_loop(0, 4, g1_own, 0)
    wait(pending[:1])
    lax.fori_loop(0, 4, g1_pair, 0)
    low, high = pl.ds(0, 4), pl.ds(4, 4)
    pending_x = [
        send(g1_sum.at[low, :, :, lanes(p)], g1_first_x.at[x], at_plane((p, y))) for p in ring_peers(x)
    ]
    g1_first_x[x] = g1_sum[0:4, :, :, lanes(x)]
    lax.fori_loop(4, 8, g1_own, 0)
    wait(pending[1:])
    lax.fori_loop(4, 8, g1_pair, 0)
    pending_y = [send(g1_sum.at[high, p], g1_first_y.at[y], at_plane((x, p))) for p in ring_peers(y)]
    g1_first_y[y] = g1_sum[4:8, y]

    bias_one_sum = jnp.sum(slope_one[...].astype(F32), axis=0, keepdims=True)
    for i in range(4):
        bias_mine[i : i + 1, :] = bias_one_sum[:, i * 128 : (i + 1) * 128]
        bias_mine[4 + i : 5 + i, :] = bias_two_sum[:, i * 128 : (i + 1) * 128]
    pending_bias = [send(bias_mine, bias_core, sibling)]

    wait(pending_g2)
    total = tree_sum([g2_plane[p].astype(F32) for p in range(16)])
    g2_piece[...] = total.astype(BF16)
    pending_g2 = [send(g2_piece.at[rows(p, 16), :], g2_z.at[z], at_z(p)) for p in z_peers]
    g2_z[z] = g2_piece[rows(z, 16), :]
    wait(pending_g2)
    total = tree_sum([g2_z[p].astype(F32) for p in range(Z)])
    g2_row[rows(z, 16), :] = total.astype(BF16)
    pending_g2 = [send(g2_row.at[rows(z, 16), :], g2_row.at[rows(z, 16), :], at_z(p)) for p in z_peers]
    wait(pending_bias)
    bias_pair[...] = bias_mine[...] + bias_core[...]
    pending_bias = [send(bias_pair, bias_x.at[x], at_plane((p, y))) for p in ring_peers(x)]
    bias_x[x] = bias_pair[...]

    wait(pending_x)

    def g1_over_x(t, carry):
        total = tree_sum([g1_first_x[p, t].astype(F32) for p in range(4)])
        g1_part_x[t] = total.astype(BF16)
        return carry

    lax.fori_loop(0, 4, g1_over_x, 0)
    pending_x = [send(g1_part_x.at[:, p], g1_then_y.at[y], at_plane((x, p))) for p in ring_peers(y)]
    g1_then_y[y] = g1_part_x[:, y]
    wait(pending_y)

    def g1_over_y(t, carry):
        total = tree_sum([g1_first_y[p, t].astype(F32) for p in range(4)])
        g1_part_y[t] = total.astype(BF16)
        return carry

    lax.fori_loop(0, 4, g1_over_y, 0)
    pending_y = [
        send(g1_part_y.at[:, :, lanes(p)], g1_then_x.at[x], at_plane((p, y))) for p in ring_peers(x)
    ]
    g1_then_x[x] = g1_part_y[:, :, lanes(x)]
    wait(pending_bias)
    bias_row[...] = tree_sum([bias_x[p] for p in range(4)])
    pending_bias = [send(bias_row, bias_y.at[y], at_plane((x, p))) for p in ring_peers(y)]
    bias_y[y] = bias_row[...]
    wait(pending_g2)
    pending_g2 = [
        send(g2_row, out_two.at[core, rows(y, 128), lanes(x)], at_plane(p)) for p in plane_peers
    ]
    out_two[core, rows(y, 128), lanes(x)] = g2_row[...]
    wait(pending_x)
    wait(pending_y)

    def g1_chips(t, carry):
        g1_piece[t] = tree_sum([g1_then_y[p, t].astype(F32) for p in range(4)]).astype(BF16)
        g1_piece[4 + t] = tree_sum([g1_then_x[p, t].astype(F32) for p in range(4)]).astype(BF16)
        return carry

    lax.fori_loop(0, 4, g1_chips, 0)
    pending = [send(g1_piece.at[p], g1_z.at[z], at_z(p)) for p in z_peers]
    g1_z[z] = g1_piece[z]
    wait(pending_bias)
    bias_chips[...] = tree_sum([bias_y[p] for p in range(4)])
    pending_bias = [send(bias_chips, bias_z.at[z], at_z(p)) for p in z_peers]
    bias_z[z] = bias_chips[...]
    wait(pending)
    total = tree_sum([g1_z[p].astype(F32) for p in range(Z)])
    out_one[core, rows(y, 32), lanes(x)] = total.astype(BF16)

    mine = out_one.at[core, rows(y, 32), lanes(x)]
    pending = [send(mine, mine, at_plane(p)) for p in plane_peers]
    wait(pending_g2)
    pending_g2 = [send(out_two.at[core], out_two.at[core], sibling)]
    wait(pending_bias)
    total = tree_sum([bias_z[p] for p in range(Z)])
    for i in range(4):
        result_bias_one[:, i * 128 : (i + 1) * 128] = total[i : i + 1, :]
        result_bias_two[:, i * 128 : (i + 1) * 128] = total[4 + i : 5 + i, :]
    wait(pending)
    pending = [send(out_one.at[core], out_one.at[core], sibling)]
    wait(pending_g2)
    stores = [
        pltpu.make_async_copy(out_two.at[0], result_self_two, load_sem.at[0]),
        pltpu.make_async_copy(out_two.at[1], result_neigh_two, load_sem.at[1]),
        pltpu.make_async_copy(out_one.at[0], result_self_one, load_sem.at[2]),
        pltpu.make_async_copy(out_one.at[1], result_neigh_one, load_sem.at[3]),
    ]
    stores[0].start()
    stores[1].start()
    wait(pending)
    stores[2].start()
    stores[3].start()
    for store in stores:
        store.wait()
    assert len(used) <= N_COPIES


def training_step(*operands):
    bf16 = [
        jnp.int32,
        jnp.int32,
        (2, 128, HID),
        (2, HID, HID),
        (2 * Z * COLS, OWN),
        (SOURCES, COLS),
        jnp.int32,
        None,
        (HID, HID),
        (HID, HID),
        None,
        (OWN_SEEDS, HID),
        jnp.int32,
        jnp.int32,
        None,
        None,
        None,
        None,
        (Z - 1, OWN, COLS),
        (2 * COLS, HID),
        (Z, 2 * COLS, HID),
        (OWN, 2 * Z * COLS),
        (OWN, HID),
        (4 * OWN, 128),
        (4 * OWN, SEEDS),
        (SEEDS, 128),
        (Z, OWN_SEEDS, 128),
        (OWN_SEEDS, HID),
        (OWN_SEEDS, HID),
        (OWN_SEEDS, HID),
        (SEEDS, 128),
        None,
        (4 * OWN, 128),
        (OWN, HID),
        (OWN, HID),
        None,
        (HID, HID),
        (HID, HID),
        (HID, HID),
        (16, 128, 128),
        (128, 128),
        (Z, 16, 128),
        (128, 128),
        None,
        (Z, 128, HID),
        (Z, 128, HID),
        (Z, 4, 32, HID),
        (4, 4, 4, 32, 128),
        (4, 4, 32, 128),
        (4, 4, 32, 128),
        (4, 4, 32, HID),
        (4, 32, HID),
        (4, 4, 32, 128),
        (Z, 32, 128),
        (Z, 32, 128),
    ]
    wide = iter(
        [
            (1, HID),
            (1, HID),
            (MIDDLE, 128),
            (SEEDS, 128),
            (SOURCES + 8, COLS),
            (OWN, COLS),
            (OWN_SEEDS, HID),
            (HID, HID),
            (Z, 128, HID),
        ]
    )
    whole = iter([(FAN_ONE, 1, MIDDLE), (FAN_ONE, MIDDLE), (1, MIDDLE), (FAN_TWO, SEEDS), (1, SEEDS)])
    scratch = [[pltpu.SMEM((MIDDLE,), jnp.int32) for k in range(FAN_ONE)]]
    for entry in bf16:
        if entry is None:
            scratch.append(pltpu.VMEM(next(wide), F32))
        elif entry is jnp.int32:
            scratch.append(pltpu.VMEM(next(whole), jnp.int32))
        else:
            scratch.append(pltpu.VMEM(entry, BF16))
    tile = (8, 128)
    four = (4, *tile)
    scratch += [pltpu.VMEM(s, F32) for s in (tile, tile, tile, four, tile, four, tile, (Z, *tile))]
    scratch += [pltpu.SemaphoreType.DMA((N_COPIES,)), pltpu.SemaphoreType.DMA((N_COPIES,))]
    scratch += [pltpu.SemaphoreType.DMA((15 + FAN_ONE,))]
    return pl.pallas_call(
        step_kernel,
        name="training_step",
        out_shape=(
            jax.ShapeDtypeStruct((128, HID), BF16),
            jax.ShapeDtypeStruct((128, HID), BF16),
            jax.ShapeDtypeStruct((HID, HID), BF16),
            jax.ShapeDtypeStruct((HID, HID), BF16),
            jax.ShapeDtypeStruct((1, HID), F32),
            jax.ShapeDtypeStruct((1, HID), F32),
        ),
        in_specs=[HBM] * len(operands),
        out_specs=(HBM, HBM, HBM, HBM, VMEM, VMEM),
        scratch_shapes=scratch,
        compiler_params=pltpu.CompilerParams(
            collective_id=0, has_side_effects=True, vmem_limit_bytes=60 << 20
        ),
    )(*operands)


def widen_kernel(*refs):
    half = len(refs) // 2
    for narrow, wide in zip(refs[:half], refs[half:]):
        wide[...] = narrow[...].astype(F32)


def widen_all(*arrays):
    steps = 2
    specs = [
        pl.BlockSpec((a.shape[0] // steps, HID), lambda i: (i, 0))
        if a.shape[0] > 1
        else pl.BlockSpec((1, HID), lambda i: (0, 0))
        for a in arrays
    ]
    return pl.pallas_call(
        widen_kernel,
        name="widen",
        grid=(steps,),
        out_shape=[jax.ShapeDtypeStruct(a.shape, F32) for a in arrays],
        in_specs=specs,
        out_specs=specs,
        compiler_params=pltpu.CompilerParams(vmem_limit_bytes=60 << 20),
    )(*arrays)


def on_device(
    features,
    nbr_one,
    count_one,
    nbr_two,
    count_two,
    self_one,
    neigh_one,
    bias_one,
    self_two,
    neigh_two,
    bias_two,
    cotangent,
):
    sums = training_step(
        nbr_one,
        features,
        count_one[None, :],
        self_one,
        neigh_one,
        bias_one[None, :],
        self_two,
        neigh_two,
        bias_two[None, :],
        cotangent,
        nbr_two,
        count_two[None, :],
    )
    g_self_one, g_neigh_one, g_self_two, g_neigh_two, g_bias_one, g_bias_two = widen_all(*sums)
    return (
        g_self_one,
        g_neigh_one,
        g_bias_one.reshape(HID),
        g_self_two,
        g_neigh_two,
        g_bias_two.reshape(HID),
    )


def solution(mesh):
    in_specs = (
        P("batch", "feat"),
        P(None, "batch"),
        P("batch"),
        P(None, "batch"),
        P("batch"),
        P("feat", None),
        P("feat", None),
        P(),
        P(),
        P(),
        P(),
        P(("batch", "feat"), None),
    )
    out_specs = (P("feat", None), P("feat", None), P(), P(), P(), P())
    return jax.shard_map(
        on_device, mesh=mesh, in_specs=in_specs, out_specs=out_specs, check_vma=False
    )
```
